32 devices in a mesh: group: 2 (over x), serve: 8 (over z, y), tensor: 2 (over core).
Axes of the slice: x: 2, y: 2, z: 4, core: 2. Of those that a mesh axis runs over, the one named last changes fastest.
Arguments:
- tokens: bfloat16 [2048, 8192], P(('group', 'serve'), 'tensor'), parts along dimension 0, may hold values from -70 to 70
- query_weight: bfloat16 [8192, 512], P(None, 'tensor'), may hold values from -0.0625 to 0.0625
- key_value_weight: bfloat16 [8192, 256], P(None, 'tensor'), may hold values from -0.0625 to 0.0625
- output_weight: bfloat16 [512, 8192], P('tensor'), may hold values from -0.25 to 0.25
- adapter_down_maps: bfloat16 [32, 48, 8192], P(('group', 'serve'), None, 'tensor'), parts along dimension 0, may hold values from -0.0625 to 0.0625
- adapter_query_up: bfloat16 [32, 16, 512], P(('group', 'serve'), None, 'tensor'), parts along dimension 0, may hold values from -1.5 to 1.5
- adapter_key_value_up: bfloat16 [32, 16, 256], P(('group', 'serve'), None, 'tensor'), parts along dimension 0, may hold values from -1.5 to 1.5
- adapter_output_down: bfloat16 [32, 16, 512], P(('group', 'serve'), None, 'tensor'), parts along dimension 0, may hold values from -0.25 to 0.25
- adapter_output_up: bfloat16 [32, 16, 8192], P(('group', 'serve'), None, 'tensor'), parts along dimension 0, may hold values from -1.5 to 1.5
- request_adapter: int32 [16], P('group'), parts along dimension 0, may hold values from 0 to 15, as said below
- adapter_pool_row: int32 [32], P('group'), parts along dimension 0, may hold values from 0 to 15, as said below
- lengths: int32 [16], P(('group', 'serve')), parts along dimension 0, may hold values from 16 to 128
Outputs:
- attention_out: bfloat16 [2048, 8192], P(('group', 'serve'), 'tensor'), parts along dimension 0
The draws below stay inside these ranges and needn't reach their ends.
There are 2 independent parts, one for each index of `group`. The reference program is written for one: setup_inputs(seed, part) draws one part's arguments, and reference() takes and returns one part's arrays. A program takes and returns all parts, laid end to end along the dimension named above; an argument that names none is the same for every part. Nothing has to cross between parts.
Inputs may be any that keep to these rules, and one draw needn't show every extreme that they name: Grouping requests by adapter_pool_row[request_adapter[r]] // 2, no group holds more than 4 requests, and some group holds exactly 4. `adapter_pool_row`: each value appears once.
All inputs are finite; a program needn't handle non-finite values.
Results may differ from the reference program's by a relative error of at most 0.012.
The reference program's roundings to bfloat16 on the way count: a program that leaves them out, or rounds other values in their place, can miss the bound.
Values may be sent and summed in bfloat16 or wider, within the bound.
No kernel may reach another device: no remote copies, remote signals or barrier semaphores. Data moves between devices by JAX's collectives and lax.ppermute only.
A program may use at most 128 MiB of HBM per device.

```python
import jax
import jax.numpy as jnp
from jax import lax

MODEL_WIDTH = 8192
HEAD_SIZE = 128
ADAPTER_RANK = 16
QUERY_HEADS = 4
CAP = 4
LEN = 128
ADP_DEV = 2
REQUESTS = 8
ADAPTER_POOL = 16
TOKENS = 1024


def draw_tokens(key, part):
    key_base = jax.random.fold_in(jax.random.fold_in(key, 11), 0)
    base_draw = jnp.clip(jax.random.normal(key_base, (TOKENS, MODEL_WIDTH), jnp.float32), -5.0, 5.0)
    return base_draw.astype(jnp.bfloat16)


def placement_draw(key):
    key_hot, key_seat, key_mix, key_local, key_slot = jax.random.split(jax.random.fold_in(key, 23), 5)
    seats_total = REQUESTS * CAP
    hot_owner = jax.random.randint(key_hot, (), 0, REQUESTS)
    seat_index = jnp.arange(seats_total, dtype=jnp.int32)
    seat_owner = seat_index // CAP
    scores = jax.random.permutation(key_seat, seats_total).astype(jnp.int32)
    scores = jnp.where(seat_owner == hot_owner, -1 - seat_index % CAP, scores)
    taken = jnp.argsort(scores, stable=True)[:REQUESTS]
    request_owner = jax.random.permutation(key_mix, seat_owner[taken])
    local_pick = jax.random.randint(key_local, (REQUESTS,), 0, ADP_DEV)
    wanted = request_owner * ADP_DEV + local_pick
    slot_table = jax.random.permutation(key_slot, ADAPTER_POOL).astype(jnp.int32)
    inverse = jnp.argsort(slot_table)
    return (slot_table, inverse[wanted].astype(jnp.int32))


def draw_request_adapter(key, part):
    return placement_draw(key)[1]


def draw_adapter_pool_row(key, part):
    return placement_draw(key)[0]


def touch_ends(array, key, low, top_value):
    longest = array.shape.index(max(array.shape))
    spots = []
    for shift in (0, 1):
        where = [jax.random.randint(jax.random.fold_in(key, axis), (), 0, length) for axis, length in enumerate(array.shape)]
        where[longest] = (where[longest] + shift) % array.shape[longest]
        spots.append(tuple(where))
    return array.at[spots[0]].set(low).at[spots[1]].set(top_value)


def levels(stream_key, dims, shards, smallest, top_value):
    loudness, own = 1.0, jax.random.fold_in(stream_key, 6)
    for position, shards_of in shards:
        heights = jnp.exp(jax.random.uniform(jax.random.fold_in(own, position), (shards_of,), jnp.float32, smallest / len(shards), top_value / len(shards)))
        loudness = loudness * jnp.repeat(heights, dims[position] // shards_of).reshape([-1 if axis == position else 1 for axis in range(len(dims))])
    return loudness


def bell_draw(own_key, extent, scale, bound, cuts=(), kind=jnp.bfloat16):
    array = jax.random.normal(own_key, extent, jnp.float32) * scale
    if len(cuts) > 0:
        array = levels(own_key, extent, cuts, -0.22, 0.18) * array
    return jnp.clip(array, min=-bound, max=bound).astype(kind)


def setup_inputs(seed: int = 0, part: int = 0) -> dict:
    streams_of = jax.random.split(jax.random.key(seed), 13)
    part_keys = jax.random.split(jax.random.fold_in(streams_of[12], part), 13)
    tokens = draw_tokens(jax.random.fold_in(jax.random.fold_in(streams_of[12], part), 71), part)
    query_weight = bell_draw(streams_of[1], (MODEL_WIDTH, QUERY_HEADS * HEAD_SIZE), MODEL_WIDTH ** -0.5, 0.0625, ((1, 2),))
    key_value_weight = bell_draw(streams_of[2], (MODEL_WIDTH, 2 * HEAD_SIZE), MODEL_WIDTH ** -0.5, 0.0625, ((1, 2),))
    output_weight = bell_draw(streams_of[3], (QUERY_HEADS * HEAD_SIZE, MODEL_WIDTH), (QUERY_HEADS * HEAD_SIZE) ** -0.5, 0.25, ((0, 2),))
    adapter_down_maps = bell_draw(part_keys[4], (ADAPTER_POOL, 3 * ADAPTER_RANK, MODEL_WIDTH), MODEL_WIDTH ** -0.5, 0.0625, ((0, 8), (2, 2)))
    adapter_query_up = bell_draw(part_keys[5], (ADAPTER_POOL, ADAPTER_RANK, QUERY_HEADS * HEAD_SIZE), ADAPTER_RANK ** -0.5, 1.5, ((0, 8), (2, 2)))
    adapter_key_value_up = bell_draw(part_keys[6], (ADAPTER_POOL, ADAPTER_RANK, 2 * HEAD_SIZE), ADAPTER_RANK ** -0.5, 1.5, ((0, 8), (2, 2)))
    adapter_output_down = bell_draw(part_keys[7], (ADAPTER_POOL, ADAPTER_RANK, QUERY_HEADS * HEAD_SIZE), (QUERY_HEADS * HEAD_SIZE) ** -0.5, 0.25, ((0, 8), (2, 2)))
    adapter_output_up = bell_draw(part_keys[8], (ADAPTER_POOL, ADAPTER_RANK, MODEL_WIDTH), ADAPTER_RANK ** -0.5, 1.5, ((0, 8), (2, 2)))
    request_adapter = draw_request_adapter(jax.random.fold_in(jax.random.fold_in(streams_of[12], part), 71), part)
    adapter_pool_row = draw_adapter_pool_row(jax.random.fold_in(jax.random.fold_in(streams_of[12], part), 71), part)
    lengths = touch_ends(jax.random.randint(part_keys[11], (REQUESTS,), LEN // 8, LEN + 1), jax.random.fold_in(part_keys[11], 1), LEN // 8, LEN).astype(jnp.int32)
    return {"tokens": tokens, "query_weight": query_weight, "key_value_weight": key_value_weight, "output_weight": output_weight, "adapter_down_maps": adapter_down_maps, "adapter_query_up": adapter_query_up, "adapter_key_value_up": adapter_key_value_up, "adapter_output_down": adapter_output_down, "adapter_output_up": adapter_output_up, "request_adapter": request_adapter, "adapter_pool_row": adapter_pool_row, "lengths": lengths}


def rotate(vectors):
    rows_count, width = vectors.shape
    half_width = width // 2
    freqs = 500000.0 ** (-(jnp.arange(half_width, dtype=jnp.float32) * 2.0 / width))
    angles = jnp.arange(rows_count, dtype=jnp.float32)[:, None] * freqs[None, :]
    cosine = jnp.cos(angles)
    sine_part = jnp.sin(angles)
    first = vectors[:, :half_width]
    second = vectors[:, half_width:]
    return jnp.concatenate([first * cosine - second * sine_part, second * cosine + first * sine_part], axis=1)


def attend(query_rows, key_rows, value_rows, length):
    rows_count = query_rows.shape[0]
    scores = jnp.dot(query_rows, key_rows.T, preferred_element_type=jnp.float32) * (query_rows.shape[1] ** -0.5)
    positions = jnp.arange(rows_count)
    allowed = (positions[None, :] <= positions[:, None]) & (positions[None, :] < length)
    scores = jnp.where(allowed, scores, -1e30)
    highest = jnp.max(scores, axis=1, keepdims=True)
    expo = jnp.exp(scores - highest)
    weights = (expo / jnp.sum(expo, axis=1, keepdims=True)).astype(jnp.bfloat16)
    return jnp.dot(weights, value_rows, preferred_element_type=jnp.float32).astype(jnp.bfloat16)


def reference(tokens, query_weight, key_value_weight, output_weight, adapter_down_maps, adapter_query_up, adapter_key_value_up, adapter_output_down, adapter_output_up, request_adapter, adapter_pool_row, lengths):
    heads = query_weight.shape[1] // HEAD_SIZE
    half_cols = heads * HEAD_SIZE // 2

    def one_request(request):
        x_rows = lax.dynamic_slice_in_dim(tokens, request * LEN, LEN, 0)
        pool_slot = adapter_pool_row[request_adapter[request]]
        down_map_rows = adapter_down_maps[pool_slot]
        query_up_map = adapter_query_up[pool_slot]
        key_value_up = adapter_key_value_up[pool_slot]
        output_down = adapter_output_down[pool_slot]
        output_up = adapter_output_up[pool_slot]
        length = lengths[request]
        shrink = jnp.dot(x_rows, down_map_rows.T, preferred_element_type=jnp.float32).astype(jnp.bfloat16)
        query_all = jnp.dot(x_rows, query_weight, preferred_element_type=jnp.float32) + jnp.dot(shrink[:, :ADAPTER_RANK], query_up_map, preferred_element_type=jnp.float32)
        key_part = jnp.dot(x_rows, key_value_weight[:, :HEAD_SIZE], preferred_element_type=jnp.float32) + jnp.dot(shrink[:, ADAPTER_RANK:2 * ADAPTER_RANK], key_value_up[:, :HEAD_SIZE], preferred_element_type=jnp.float32)
        value_part = jnp.dot(x_rows, key_value_weight[:, HEAD_SIZE:], preferred_element_type=jnp.float32) + jnp.dot(shrink[:, 2 * ADAPTER_RANK:3 * ADAPTER_RANK], key_value_up[:, HEAD_SIZE:], preferred_element_type=jnp.float32)
        key_rounded = lax.optimization_barrier(key_part.astype(jnp.bfloat16))
        key_rows = rotate(key_rounded.astype(jnp.float32)).astype(jnp.bfloat16)
        value_rows = value_part.astype(jnp.bfloat16)
        attended_list = []
        for head in range(heads):
            query_rows = rotate(query_all[:, head * HEAD_SIZE:(head + 1) * HEAD_SIZE]).astype(jnp.bfloat16)
            attended_list.append(attend(query_rows, key_rows, value_rows, length))
        attended_all = jnp.concatenate(attended_list, axis=1)
        base_total = jnp.zeros((LEN, MODEL_WIDTH), jnp.float32)
        for half in range(2):
            term = jnp.dot(attended_all[:, half * half_cols:(half + 1) * half_cols], output_weight[half * half_cols:(half + 1) * half_cols], preferred_element_type=jnp.float32)
            term = lax.optimization_barrier(term.astype(jnp.bfloat16))
            base_total = base_total + term.astype(jnp.float32)
        low = jnp.dot(attended_all, output_down.T, preferred_element_type=jnp.float32).astype(jnp.bfloat16)
        delta_out = jnp.dot(low, output_up, preferred_element_type=jnp.float32)
        valid_rows = (jnp.arange(LEN) < length)[:, None]
        return jnp.where(valid_rows, base_total + delta_out, 0.0).astype(jnp.bfloat16)

    results = lax.map(one_request, jnp.arange(REQUESTS, dtype=jnp.int32))
    return results.reshape(TOKENS, MODEL_WIDTH)
```

```python
import functools

import jax
import jax.numpy as jnp
import numpy as np
from jax import lax
from jax.experimental import pallas as pl
from jax.experimental.pallas import tpu as pltpu
from jax.sharding import PartitionSpec as P

HEAD_SIZE = 128
MIB = 1 << 20
VMEM = pl.BlockSpec(memory_space=pltpu.VMEM)
SMEM = pl.BlockSpec(memory_space=pltpu.SMEM)
ANY = pl.BlockSpec(memory_space=pl.ANY)


def span(bits):
    masks = [0]
    for bit in bits:
        masks += [mask ^ bit for mask in masks]
    return masks


def params(mib):
    return pltpu.CompilerParams(vmem_limit_bytes=mib * MIB)


def cost(flops, bytes_accessed):
    return pl.CostEstimate(flops=flops, transcendentals=0, bytes_accessed=bytes_accessed)


class Route:
    def __init__(self, part, order, devices, request_adapter, adapter_pool_row):
        self.parts, self.masks = [part], [0]
        self.packets, self.known = [], []
        self.bits = [1 << bit for bit in order]
        self.done = 0
        self.devices = devices
        self.tables = (request_adapter, adapter_pool_row)
        self.held = part.shape[0]

    def arrays(self):
        return self.parts + self.packets

    def choose(self, tables, refs, slot, store):
        requests, pool = tables
        here = lax.axis_index("serve")
        wanted = pool[requests[here ^ slot]]
        offset = (wanted // self.held) ^ here
        for ref, mask in zip(refs, self.masks):

            @pl.when(offset == mask)
            def _(ref=ref):
                store(ref, wanted % self.held)

        for ref, (masks, slots) in zip(refs[len(self.masks):], self.known):
            arrived = functools.reduce(lambda a, b: a | b, [offset == mask for mask in masks])

            @pl.when(arrived)
            def _(ref=ref, slots=slots):
                store(ref, slots.index(slot))

    def step(self, after=()):
        bit = self.bits[self.done]
        slots = span(self.bits[self.done + 1:])
        pairs = [(i, i ^ bit) for i in range(self.devices)]
        out = None
        if not self.known and self.held * len(self.parts) <= len(slots):
            self.parts += [lax.ppermute(part, "serve", pairs) for part in self.parts]
            self.masks += [mask ^ bit for mask in self.masks]
        else:
            out = self.pick([bit ^ slot for slot in slots], after)
            self.packets.append(lax.ppermute(out, "serve", pairs))
            self.known.append(([bit ^ mask for mask in span(self.bits[:self.done])], slots))
        self.done += 1
        return out

    def pick(self, slots, after):
        arrays = self.arrays()
        shape = (len(slots),) + arrays[0].shape[1:]

        def kernel(requests, pool, *refs):
            out = refs[-1]
            for place, slot in enumerate(slots):
                out[place] = refs[0][0]

                def store(ref, index, place=place):
                    out[place] = ref[index]

                self.choose((requests, pool), refs, slot, store)

        return pl.pallas_call(
            kernel,
            in_specs=[SMEM, SMEM] + [VMEM] * len(arrays) + [ANY] * len(after),
            out_specs=VMEM,
            out_shape=jax.ShapeDtypeStruct(shape, arrays[0].dtype),
            compiler_params=params(4),
            cost_estimate=cost(0, 4 * int(np.prod(shape))),
            name="pick",
        )(*self.tables, *arrays, *after)


def base_kernel(tensor, own_tokens, other_tokens, query_weight, key_value_weight, out):
    step = pl.program_id(0)
    steps = pl.num_programs(0)
    width = query_weight.shape[1]

    @pl.when(step == 0)
    def _():
        out[...] = jnp.zeros_like(out)

    def add(rows):
        out[:, :width] += jnp.dot(rows[...], query_weight[...], preferred_element_type=jnp.float32)
        out[:, width:] += jnp.dot(rows[...], key_value_weight[...], preferred_element_type=jnp.float32)

    @pl.when(step < steps // 2)
    def _():
        add(own_tokens)

    @pl.when(step >= steps // 2)
    def _():
        add(other_tokens)


def base_products(tensor, own_tokens, other_tokens, query_weight, key_value_weight):
    rows, half = own_tokens.shape
    blocks = 4
    depth = half // blocks
    columns = query_weight.shape[1] + key_value_weight.shape[1]

    def weight_block(step, tensor):
        own = step < blocks
        return (jnp.where(own, tensor[0], 1 - tensor[0]) * blocks + step % blocks, 0)

    return pl.pallas_call(
        base_kernel,
        grid_spec=pltpu.PrefetchScalarGridSpec(
            num_scalar_prefetch=1,
            grid=(2 * blocks,),
            in_specs=[
                pl.BlockSpec((rows, depth), lambda i, t: (0, jnp.minimum(i, blocks - 1))),
                pl.BlockSpec((rows, depth), lambda i, t: (0, jnp.maximum(i - blocks, 0))),
                pl.BlockSpec((depth, query_weight.shape[1]), weight_block),
                pl.BlockSpec((depth, key_value_weight.shape[1]), weight_block),
            ],
            out_specs=pl.BlockSpec((rows, columns), lambda i, t: (0, 0)),
        ),
        out_shape=jax.ShapeDtypeStruct((rows, columns), jnp.float32),
        compiler_params=params(8),
        cost_estimate=cost(4 * rows * half * columns, 4 * half * (rows + columns)),
        name="base",
    )(tensor, own_tokens, other_tokens, query_weight, key_value_weight)


def shrink_partial(routes, tokens, small_width):
    rows, half = tokens.shape
    rank = routes[0].parts[0].shape[1]
    counts = [len(route.arrays()) for route in routes]
    arrays = sum([route.arrays() for route in routes], [])

    def kernel(requests, pool, rows_ref, *refs):
        inputs, (out, small) = refs[:-2 - len(routes)], refs[-2 - len(routes):-len(routes)]
        held = refs[-len(routes):]
        at = 0
        for place, (route, count) in enumerate(zip(routes, counts)):

            def store(ref, index, place=place):
                held[place][...] = ref[index]

            route.choose((requests, pool), inputs[at:at + count], 0, store)
            at += count
        for place in range(len(routes)):
            out[:, place * rank:(place + 1) * rank] = lax.dot_general(
                rows_ref[...], held[place][:, :half], (((1,), (1,)), ((), ())),
                preferred_element_type=jnp.float32)
        small[...] = held[0][:, half:]

    return pl.pallas_call(
        kernel,
        in_specs=[SMEM, SMEM] + [VMEM] * (1 + len(arrays)),
        out_specs=(VMEM, VMEM),
        out_shape=(
            jax.ShapeDtypeStruct((rows, rank * len(routes)), jnp.float32),
            jax.ShapeDtypeStruct((rank, small_width), tokens.dtype),
        ),
        scratch_shapes=[pltpu.VMEM(route.parts[0].shape[1:], tokens.dtype) for route in routes],
        compiler_params=params(6),
        cost_estimate=cost(2 * rows * half * rank * len(routes), 2 * rows * half),
        name="shrink",
    )(*routes[0].tables, tokens, *arrays)


def rotary_tables(rows, width):
    half = width // 2
    freqs = np.float32(500000.0) ** (-(np.arange(half, dtype=np.float32) * np.float32(2.0) / np.float32(width)))
    angles = np.arange(rows, dtype=np.float32)[:, None] * freqs.astype(np.float32)[None, :]
    cosine, sine = np.cos(angles), np.sin(angles)
    return (
        np.concatenate([cosine, cosine], axis=1).astype(np.float32),
        np.concatenate([-sine, sine], axis=1).astype(np.float32),
    )


def attention_kernel(
    place, base_own, base_other, shrink_own, shrink_other, small_own, small_other, cosine, sine,
    weight_own, weight_other, out, low_out, *, query_columns, key_columns,
):
    tensor, length = place[0], place[1]
    rank = small_own.shape[0]
    rows = out.shape[0]
    size = HEAD_SIZE
    shrink = (shrink_own[...] + shrink_other[...]).astype(jnp.bfloat16)
    first = tensor == 0

    def up(part, base, small, start, base_start, width):
        return base[:, base_start:base_start + width] + jnp.dot(
            part, small[:, start:start + width], preferred_element_type=jnp.float32)

    def rotate(v):
        return v * cosine[...] + pltpu.roll(v, size // 2, 1) * sine[...]

    own_side = shrink[:, rank:2 * rank], shrink[:, 2 * rank:3 * rank]
    own_part = jnp.where(first, own_side[0], own_side[1])
    other_part = jnp.where(first, own_side[1], own_side[0])
    own_kv = up(own_part, base_own, small_own, query_columns, query_columns, key_columns).astype(jnp.bfloat16)
    other_kv = up(other_part, base_other, small_other, query_columns, query_columns, key_columns).astype(jnp.bfloat16)
    keys = jnp.where(first, own_kv, other_kv)
    values = jnp.where(first, other_kv, own_kv)
    keys = rotate(keys.astype(jnp.float32)).astype(jnp.bfloat16)

    at = lax.broadcasted_iota(jnp.int32, (rows, rows), 0)
    to = lax.broadcasted_iota(jnp.int32, (rows, rows), 1)
    allowed = (to <= at) & (to < length)

    def heads(base, small):
        queries = up(shrink[:, :rank], base, small, 0, 0, query_columns)
        done = []
        for start in range(0, query_columns, size):
            query = rotate(queries[:, start:start + size]).astype(jnp.bfloat16)
            scores = lax.dot_general(
                query, keys, (((1,), (1,)), ((), ())), preferred_element_type=jnp.float32) * size ** (-0.5)
            scores = jnp.where(allowed, scores, -1e30)
            expo = jnp.exp(scores - jnp.max(scores, axis=1, keepdims=True))
            weights = (expo / jnp.sum(expo, axis=1, keepdims=True)).astype(jnp.bfloat16)
            done.append(jnp.dot(weights, values, preferred_element_type=jnp.float32).astype(jnp.bfloat16))
        return jnp.concatenate(done, axis=1)

    attended_own = heads(base_own, small_own)
    attended_other = heads(base_other, small_other)

    def down(attended, small):
        return lax.dot_general(
            attended, small[:, query_columns + key_columns:], (((1,), (1,)), ((), ())),
            preferred_element_type=jnp.float32)

    low_out[...] = (down(attended_own, small_own) + down(attended_other, small_other)).astype(jnp.bfloat16)
    columns = out.shape[1]
    tile = 512
    for start in range(0, columns, tile):
        cut = slice(start, start + tile)
        own = jnp.dot(attended_own, weight_own[:, cut], preferred_element_type=jnp.float32)
        other = jnp.dot(attended_other, weight_other[:, cut], preferred_element_type=jnp.float32)
        out[:, cut] = own.astype(jnp.bfloat16).astype(jnp.float32) + other.astype(jnp.bfloat16).astype(jnp.float32)


def attention(place, base, shrink, small, weight, query_columns, key_columns):
    rows = base[0].shape[0]
    columns = weight[0].shape[1]
    rank = small[0].shape[0]
    cosine, sine = rotary_tables(rows, HEAD_SIZE)
    operands = (*base, *shrink, *small, cosine, sine, *weight)
    return pl.pallas_call(
        functools.partial(attention_kernel, query_columns=query_columns, key_columns=key_columns),
        in_specs=[SMEM] + [VMEM] * len(operands),
        out_specs=(VMEM, VMEM),
        out_shape=(
            jax.ShapeDtypeStruct((rows, columns), jnp.float32),
            jax.ShapeDtypeStruct((rows, rank), jnp.bfloat16),
        ),
        compiler_params=params(16),
        cost_estimate=cost(4 * rows * query_columns * columns, 4 * query_columns * columns),
        name="attention",
    )(place, *operands)


def finish(route, place, base, low):
    rows, columns = base.shape
    arrays = route.arrays()

    def kernel(requests, pool, place, base_ref, low_ref, *refs):
        inputs, out, held = refs[:len(arrays)], refs[-2], refs[-1]

        def store(ref, index):
            held[...] = ref[index]

        route.choose((requests, pool), inputs, 0, store)
        valid = lax.broadcasted_iota(jnp.int32, (rows, 1), 0) < place[1]
        tile = 512
        for start in range(0, columns, tile):
            cut = slice(start, start + tile)
            delta = jnp.dot(low_ref[...], held[:, cut], preferred_element_type=jnp.float32)
            out[:, cut] = jnp.where(valid, base_ref[:, cut] + delta, 0.0).astype(out.dtype)

    return pl.pallas_call(
        kernel,
        in_specs=[SMEM, SMEM, SMEM] + [VMEM] * (2 + len(arrays)),
        out_specs=VMEM,
        out_shape=jax.ShapeDtypeStruct((rows, columns), jnp.bfloat16),
        scratch_shapes=[pltpu.VMEM(arrays[0].shape[1:], arrays[0].dtype)],
        compiler_params=params(8),
        cost_estimate=cost(2 * rows * low.shape[1] * columns, 6 * rows * columns),
        name="finish",
    )(*route.tables, place, base, low, *arrays)


def orders(bits):
    each = list(range(bits))
    first = each
    second = [1, 0] + each[2:] if bits > 1 else each
    third = [each[-1]] + each[:-1]
    return first, second, third


def local(
    devices,
    tokens,
    query_weight,
    key_value_weight,
    output_weight,
    adapter_down_maps,
    adapter_query_up,
    adapter_key_value_up,
    adapter_output_down,
    adapter_output_up,
    request_adapter,
    adapter_pool_row,
    lengths,
):
    tensor = lax.axis_index("tensor")
    pair = [(0, 1), (1, 0)]
    half = tokens.shape[1]
    rank = adapter_query_up.shape[1]
    query_columns = query_weight.shape[1]
    key_columns = key_value_weight.shape[1]
    place = jnp.stack([tensor, lengths[0]]).astype(jnp.int32)

    def swap(x):
        return lax.ppermute(x, "tensor", pair)

    small = jnp.concatenate([adapter_query_up, adapter_key_value_up, adapter_output_down], axis=2)
    first, second, third = orders(devices.bit_length() - 1)

    def route(part, order):
        return Route(part, order, devices, request_adapter, adapter_pool_row)

    down = [adapter_down_maps[:, i * rank:(i + 1) * rank] for i in range(3)]
    routes = [
        route(jnp.concatenate([down[0], small], axis=2), first),
        route(down[1], second),
        route(down[2], third),
    ]
    up_route = route(adapter_output_up, first)
    for _ in range(devices.bit_length() - 1):
        for each in (*routes, up_route):
            each.step()

    other_tokens = swap(tokens)
    base_own = base_products(place, tokens, other_tokens, query_weight, key_value_weight)
    base_other = swap(base_own)
    weight_own = lax.dynamic_slice_in_dim(output_weight, tensor * half, half, 1)
    weight_other = swap(lax.dynamic_slice_in_dim(output_weight, (1 - tensor) * half, half, 1))

    shrink_own, small_own = shrink_partial(routes, tokens, small.shape[2])
    base, low = attention(
        place, (base_own, base_other), (shrink_own, swap(shrink_own)), (small_own, swap(small_own)),
        (weight_own, weight_other), query_columns, key_columns)
    return finish(up_route, place, base, low)


def solution(mesh):
    placed = (
        P(("group", "serve"), "tensor"),
        P(None, "tensor"),
        P(None, "tensor"),
        P("tensor", None),
        P(("group", "serve"), None, "tensor"),
        P(("group", "serve"), None, "tensor"),
        P(("group", "serve"), None, "tensor"),
        P(("group", "serve"), None, "tensor"),
        P(("group", "serve"), None, "tensor"),
        P("group"),
        P("group"),
        P(("group", "serve")),
    )
    return jax.shard_map(
        functools.partial(local, mesh.shape["serve"]),
        mesh=mesh,
        in_specs=placed,
        out_specs=P(("group", "serve"), "tensor"),
        check_vma=False,
    )
```

```python
import functools

import jax
import jax.numpy as jnp
import numpy as np
from jax import lax
from jax.experimental import pallas as pl
from jax.experimental.pallas import tpu as pltpu
from jax.sharding import PartitionSpec as P

HEAD_SIZE = 128
MIB = 1 << 20
VMEM = pl.BlockSpec(memory_space=pltpu.VMEM)
SMEM = pl.BlockSpec(memory_space=pltpu.SMEM)
ANY = pl.BlockSpec(memory_space=pl.ANY)


def span(bits):
    masks = [0]
    for bit in bits:
        masks += [mask ^ bit for mask in masks]
    return masks


def params(mib):
    return pltpu.CompilerParams(vmem_limit_bytes=mib * MIB)


def cost(flops, bytes_accessed):
    return pl.CostEstimate(flops=flops, transcendentals=0, bytes_accessed=bytes_accessed)


class Route:
    def __init__(self, part, order, devices, request_adapter, adapter_pool_row):
        self.parts, self.masks = [part], [0]
        self.packets, self.known = [], []
        self.bits = [1 << bit for bit in order]
        self.done = 0
        self.devices = devices
        self.tables = (request_adapter, adapter_pool_row)
        self.held = part.shape[0]

    def arrays(self):
        return self.parts + self.packets

    def choose(self, tables, refs, slot, store):
        requests, pool = tables
        here = lax.axis_index("serve")
        wanted = pool[requests[here ^ slot]]
        offset = (wanted // self.held) ^ here
        for ref, mask in zip(refs, self.masks):

            @pl.when(offset == mask)
            def _(ref=ref):
                store(ref, wanted % self.held)

        for ref, (masks, slots) in zip(refs[len(self.masks):], self.known):
            arrived = functools.reduce(lambda a, b: a | b, [offset == mask for mask in masks])

            @pl.when(arrived)
            def _(ref=ref, slots=slots):
                store(ref, slots.index(slot))

    def step(self, after=()):
        bit = self.bits[self.done]
        slots = span(self.bits[self.done + 1:])
        pairs = [(i, i ^ bit) for i in range(self.devices)]
        out = None
        if not self.known and self.held * len(self.parts) <= len(slots):
            self.parts += [lax.ppermute(part, "serve", pairs) for part in self.parts]
            self.masks += [mask ^ bit for mask in self.masks]
        else:
            out = self.pick([bit ^ slot for slot in slots], after)
            self.packets.append(lax.ppermute(out, "serve", pairs))
            self.known.append(([bit ^ mask for mask in span(self.bits[:self.done])], slots))
        self.done += 1
        return out

    def pick(self, slots, after):
        arrays = self.arrays()
        shape = (len(slots),) + arrays[0].shape[1:]

        def kernel(requests, pool, *refs):
            out = refs[-1]
            for place, slot in enumerate(slots):
                out[place] = refs[0][0]

                def store(ref, index, place=place):
                    out[place] = ref[index]

                self.choose((requests, pool), refs, slot, store)

        return pl.pallas_call(
            kernel,
            in_specs=[SMEM, SMEM] + [VMEM] * len(arrays) + [ANY] * len(after),
            out_specs=VMEM,
            out_shape=jax.ShapeDtypeStruct(shape, arrays[0].dtype),
            compiler_params=params(4),
            cost_estimate=cost(0, 4 * int(np.prod(shape))),
            name="pick",
        )(*self.tables, *arrays, *after)


def base_kernel(place, own_tokens, other_tokens, query_weight, key_value_weight, out):
    step = pl.program_id(0)
    steps = pl.num_programs(0)
    width = query_weight.shape[1]

    @pl.when(step == 0)
    def _():
        out[...] = jnp.zeros_like(out)

    def add(rows):
        out[:, :width] += jnp.dot(rows[...], query_weight[...], preferred_element_type=jnp.float32)
        out[:, width:] += jnp.dot(rows[...], key_value_weight[...], preferred_element_type=jnp.float32)

    @pl.when(step < steps // 2)
    def _():
        add(own_tokens)

    @pl.when(step >= steps // 2)
    def _():
        add(other_tokens)


def base_products(place, own_tokens, other_tokens, query_weight, key_value_weight):
    rows, half = own_tokens.shape
    blocks = 4
    depth = half // blocks
    columns = query_weight.shape[1] + key_value_weight.shape[1]

    def weight_block(step, place):
        own = step < blocks
        return (jnp.where(own, place[0], 1 - place[0]) * blocks + step % blocks, 0)

    return pl.pallas_call(
        base_kernel,
        grid_spec=pltpu.PrefetchScalarGridSpec(
            num_scalar_prefetch=1,
            grid=(2 * blocks,),
            in_specs=[
                pl.BlockSpec((rows, depth), lambda i, t: (0, jnp.minimum(i, blocks - 1))),
                pl.BlockSpec((rows, depth), lambda i, t: (0, jnp.maximum(i - blocks, 0))),
                pl.BlockSpec((depth, query_weight.shape[1]), weight_block),
                pl.BlockSpec((depth, key_value_weight.shape[1]), weight_block),
            ],
            out_specs=pl.BlockSpec((rows, columns), lambda i, t: (0, 0)),
        ),
        out_shape=jax.ShapeDtypeStruct((rows, columns), jnp.float32),
        compiler_params=params(8),
        cost_estimate=cost(4 * rows * half * columns, 4 * half * (rows + columns)),
        name="base",
    )(place, own_tokens, other_tokens, query_weight, key_value_weight)


def shrink_partial(routes, tokens, small_width):
    rows, half = tokens.shape
    rank = routes[0].parts[0].shape[1]
    counts = [len(route.arrays()) for route in routes]
    arrays = sum([route.arrays() for route in routes], [])

    def kernel(requests, pool, rows_ref, *refs):
        inputs, (out, small) = refs[:-2 - len(routes)], refs[-2 - len(routes):-len(routes)]
        held = refs[-len(routes):]
        at = 0
        for place, (route, count) in enumerate(zip(routes, counts)):

            def store(ref, index, place=place):
                held[place][...] = ref[index]

            route.choose((requests, pool), inputs[at:at + count], 0, store)
            at += count
        for place in range(len(routes)):
            out[:, place * rank:(place + 1) * rank] = lax.dot_general(
                rows_ref[...], held[place][:, :half], (((1,), (1,)), ((), ())),
                preferred_element_type=jnp.float32)
        small[...] = held[0][:, half:]

    return pl.pallas_call(
        kernel,
        in_specs=[SMEM, SMEM] + [VMEM] * (1 + len(arrays)),
        out_specs=(VMEM, VMEM),
        out_shape=(
            jax.ShapeDtypeStruct((rows, rank * len(routes)), jnp.float32),
            jax.ShapeDtypeStruct((rank, small_width), tokens.dtype),
        ),
        scratch_shapes=[pltpu.VMEM(route.parts[0].shape[1:], tokens.dtype) for route in routes],
        compiler_params=params(6),
        cost_estimate=cost(2 * rows * half * rank * len(routes), 2 * rows * half),
        name="shrink",
    )(*routes[0].tables, tokens, *arrays)


def rotary_tables(rows, width):
    half = width // 2
    freqs = np.float32(500000.0) ** (-(np.arange(half, dtype=np.float32) * np.float32(2.0) / np.float32(width)))
    angles = np.arange(rows, dtype=np.float32)[:, None] * freqs.astype(np.float32)[None, :]
    cosine, sine = np.cos(angles), np.sin(angles)
    return (
        np.concatenate([cosine, cosine], axis=1).astype(np.float32),
        np.concatenate([-sine, sine], axis=1).astype(np.float32),
    )


def attention_kernel(
    place, base_own, base_other, shrink_own, shrink_other, small_own, small_other, cosine, sine,
    weight_own, weight_other, out, low_out, held_own, held_other, sems, *, query_columns, key_columns,
):
    tensor, length = place[0], place[1]
    half = out.shape[1]
    mine = pl.ds(pl.multiple_of(tensor * half, half), half)
    fetches = [
        pltpu.make_async_copy(weight.at[:, mine], held, sems.at[i])
        for i, (weight, held) in enumerate(((weight_own, held_own), (weight_other, held_other)))
    ]
    for fetch in fetches:
        fetch.start()
    rank = small_own.shape[0]
    rows = out.shape[0]
    size = HEAD_SIZE
    shrink = (shrink_own[...] + shrink_other[...]).astype(jnp.bfloat16)
    first = tensor == 0

    def up(part, base, small, start, base_start, width):
        return base[:, base_start:base_start + width] + jnp.dot(
            part, small[:, start:start + width], preferred_element_type=jnp.float32)

    def rotate(v):
        return v * cosine[...] + pltpu.roll(v, size // 2, 1) * sine[...]

    own_side = shrink[:, rank:2 * rank], shrink[:, 2 * rank:3 * rank]
    own_part = jnp.where(first, own_side[0], own_side[1])
    other_part = jnp.where(first, own_side[1], own_side[0])
    own_kv = up(own_part, base_own, small_own, query_columns, query_columns, key_columns).astype(jnp.bfloat16)
    other_kv = up(other_part, base_other, small_other, query_columns, query_columns, key_columns).astype(jnp.bfloat16)
    keys = jnp.where(first, own_kv, other_kv)
    values = jnp.where(first, other_kv, own_kv)
    keys = rotate(keys.astype(jnp.float32)).astype(jnp.bfloat16)

    at = lax.broadcasted_iota(jnp.int32, (rows, rows), 0)
    to = lax.broadcasted_iota(jnp.int32, (rows, rows), 1)
    allowed = (to <= at) & (to < length)

    def heads(base, small):
        queries = up(shrink[:, :rank], base, small, 0, 0, query_columns)
        done = []
        for start in range(0, query_columns, size):
            query = rotate(queries[:, start:start + size]).astype(jnp.bfloat16)
            scores = lax.dot_general(
                query, keys, (((1,), (1,)), ((), ())), preferred_element_type=jnp.float32) * size ** (-0.5)
            scores = jnp.where(allowed, scores, -1e30)
            expo = jnp.exp(scores - jnp.max(scores, axis=1, keepdims=True))
            weights = (expo / jnp.sum(expo, axis=1, keepdims=True)).astype(jnp.bfloat16)
            done.append(jnp.dot(weights, values, preferred_element_type=jnp.float32).astype(jnp.bfloat16))
        return jnp.concatenate(done, axis=1)

    attended_own = heads(base_own, small_own)
    attended_other = heads(base_other, small_other)

    def down(attended, small):
        return lax.dot_general(
            attended, small[:, query_columns + key_columns:], (((1,), (1,)), ((), ())),
            preferred_element_type=jnp.float32)

    low_out[...] = (down(attended_own, small_own) + down(attended_other, small_other)).astype(jnp.bfloat16)
    for fetch in fetches:
        fetch.wait()
    tile = 512
    for start in range(0, half, tile):
        cut = slice(start, start + tile)
        own = jnp.dot(attended_own, held_own[:, cut], preferred_element_type=jnp.float32)
        other = jnp.dot(attended_other, held_other[:, cut], preferred_element_type=jnp.float32)
        out[:, cut] = own.astype(jnp.bfloat16).astype(jnp.float32) + other.astype(jnp.bfloat16).astype(jnp.float32)


def attention(place, base, shrink, small, weight, query_columns, key_columns):
    rows = base[0].shape[0]
    heads, columns = weight[0].shape[0], weight[0].shape[1] // 2
    rank = small[0].shape[0]
    cosine, sine = rotary_tables(rows, HEAD_SIZE)
    operands = (*base, *shrink, *small, cosine, sine, *weight)
    return pl.pallas_call(
        functools.partial(attention_kernel, query_columns=query_columns, key_columns=key_columns),
        in_specs=[SMEM] + [VMEM] * (len(operands) - 2) + [ANY] * 2,
        out_specs=(VMEM, VMEM),
        out_shape=(
            jax.ShapeDtypeStruct((rows, columns), jnp.float32),
            jax.ShapeDtypeStruct((rows, rank), jnp.bfloat16),
        ),
        scratch_shapes=[pltpu.VMEM((heads, columns), weight[0].dtype)] * 2 + [pltpu.SemaphoreType.DMA((2,))],
        compiler_params=params(16),
        cost_estimate=cost(4 * rows * query_columns * columns, 4 * query_columns * columns),
        name="attention",
    )(place, *operands)


def finish(route, place, base, low):
    rows, columns = base.shape
    arrays = route.arrays()

    def kernel(requests, pool, place, base_ref, low_ref, *refs):
        inputs, out, held = refs[:len(arrays)], refs[-2], refs[-1]

        def store(ref, index):
            held[...] = ref[index]

        route.choose((requests, pool), inputs, 0, store)
        valid = lax.broadcasted_iota(jnp.int32, (rows, 1), 0) < place[1]
        tile = 512
        for start in range(0, columns, tile):
            cut = slice(start, start + tile)
            delta = jnp.dot(low_ref[...], held[:, cut], preferred_element_type=jnp.float32)
            out[:, cut] = jnp.where(valid, base_ref[:, cut] + delta, 0.0).astype(out.dtype)

    return pl.pallas_call(
        kernel,
        in_specs=[SMEM, SMEM, SMEM] + [VMEM] * (2 + len(arrays)),
        out_specs=VMEM,
        out_shape=jax.ShapeDtypeStruct((rows, columns), jnp.bfloat16),
        scratch_shapes=[pltpu.VMEM(arrays[0].shape[1:], arrays[0].dtype)],
        compiler_params=params(8),
        cost_estimate=cost(2 * rows * low.shape[1] * columns, 6 * rows * columns),
        name="finish",
    )(*route.tables, place, base, low, *arrays)


def orders(bits):
    each = list(range(bits))
    first = each
    second = [1, 0] + each[2:] if bits > 1 else each
    third = [each[-1]] + each[:-1]
    return first, second, third


def local(
    devices,
    tokens,
    query_weight,
    key_value_weight,
    output_weight,
    adapter_down_maps,
    adapter_query_up,
    adapter_key_value_up,
    adapter_output_down,
    adapter_output_up,
    request_adapter,
    adapter_pool_row,
    lengths,
):
    tensor = lax.axis_index("tensor")
    pair = [(0, 1), (1, 0)]
    half = tokens.shape[1]
    rank = adapter_query_up.shape[1]
    query_columns = query_weight.shape[1]
    key_columns = key_value_weight.shape[1]
    place = jnp.stack([tensor, lengths[0]]).astype(jnp.int32)

    def swap(x):
        return lax.ppermute(x, "tensor", pair)

    small = jnp.concatenate([adapter_query_up, adapter_key_value_up, adapter_output_down], axis=2)
    first, second, third = orders(devices.bit_length() - 1)

    def route(part, order):
        return Route(part, order, devices, request_adapter, adapter_pool_row)

    down = [adapter_down_maps[:, i * rank:(i + 1) * rank] for i in range(3)]
    first_route = route(jnp.concatenate([down[0], small], axis=2), first)
    second_route = route(down[1], second)
    third_route = route(down[2], third)
    routes = [first_route, second_route, third_route]
    up_route = route(adapter_output_up, first)
    weight_other = swap(output_weight)
    other_tokens = swap(tokens)
    for each in (third_route, second_route, first_route, up_route):
        each.step()
    base_own = base_products(place, tokens, other_tokens, query_weight, key_value_weight)
    base_other = swap(base_own)
    last = None
    for turn, each in enumerate((second_route, first_route, third_route, up_route) * 2):
        if turn == 0:
            last = base_own
        sent = each.step(() if last is None else (last,))
        last = each.arrays()[-1] if sent is None else sent

    shrink_own, small_own = shrink_partial(routes, tokens, small.shape[2])
    base, low = attention(
        place, (base_own, base_other), (shrink_own, swap(shrink_own)), (small_own, swap(small_own)),
        (output_weight, weight_other), query_columns, key_columns)
    return finish(up_route, place, base, low)


def solution(mesh):
    placed = (
        P(("group", "serve"), "tensor"),
        P(None, "tensor"),
        P(None, "tensor"),
        P("tensor", None),
        P(("group", "serve"), None, "tensor"),
        P(("group", "serve"), None, "tensor"),
        P(("group", "serve"), None, "tensor"),
        P(("group", "serve"), None, "tensor"),
        P(("group", "serve"), None, "tensor"),
        P("group"),
        P("group"),
        P(("group", "serve")),
    )
    return jax.shard_map(
        functools.partial(local, mesh.shape["serve"]),
        mesh=mesh,
        in_specs=placed,
        out_specs=P(("group", "serve"), "tensor"),
        check_vma=False,
    )
```

```python
import functools

import jax
import jax.numpy as jnp
import numpy as np
from jax import lax
from jax.experimental import pallas as pl
from jax.experimental.pallas import tpu as pltpu
from jax.sharding import PartitionSpec as P

HEAD_SIZE = 128
MIB = 1 << 20
VMEM = pl.BlockSpec(memory_space=pltpu.VMEM)
SMEM = pl.BlockSpec(memory_space=pltpu.SMEM)
ANY = pl.BlockSpec(memory_space=pl.ANY)


def span(bits):
    masks = [0]
    for bit in bits:
        masks += [mask ^ bit for mask in masks]
    return masks


def params(mib):
    return pltpu.CompilerParams(vmem_limit_bytes=mib * MIB)


def cost(flops, bytes_accessed):
    return pl.CostEstimate(flops=flops, transcendentals=0, bytes_accessed=bytes_accessed)


class Route:
    def __init__(self, part, order, devices, request_adapter, adapter_pool_row):
        self.parts, self.masks = [part], [0]
        self.packets, self.known = [], []
        self.bits = [1 << bit for bit in order]
        self.done = 0
        self.devices = devices
        self.tables = (request_adapter, adapter_pool_row)
        self.held = part.shape[0]

    def arrays(self):
        return self.parts + self.packets

    def choose(self, tables, refs, slot, store):
        requests, pool = tables
        here = lax.axis_index("serve")
        wanted = pool[requests[here ^ slot]]
        offset = (wanted // self.held) ^ here
        for ref, mask in zip(refs, self.masks):

            @pl.when(offset == mask)
            def _(ref=ref):
                store(ref, wanted % self.held)

        for ref, (masks, slots) in zip(refs[len(self.masks):], self.known):
            arrived = functools.reduce(lambda a, b: a | b, [offset == mask for mask in masks])

            @pl.when(arrived)
            def _(ref=ref, slots=slots):
                store(ref, slots.index(slot))

    def step(self, after=()):
        bit = self.bits[self.done]
        slots = span(self.bits[self.done + 1:])
        pairs = [(i, i ^ bit) for i in range(self.devices)]
        out = None
        if not self.known and self.held * len(self.parts) <= len(slots):
            self.parts += [lax.ppermute(part, "serve", pairs) for part in self.parts]
            self.masks += [mask ^ bit for mask in self.masks]
        else:
            out = self.pick([bit ^ slot for slot in slots], after)
            self.packets.append(lax.ppermute(out, "serve", pairs))
            self.known.append(([bit ^ mask for mask in span(self.bits[:self.done])], slots))
        self.done += 1
        return out

    def pick(self, slots, after):
        arrays = self.arrays()
        shape = (len(slots),) + arrays[0].shape[1:]

        def kernel(requests, pool, *refs):
            out = refs[-1]
            for place, slot in enumerate(slots):
                out[place] = refs[0][0]

                def store(ref, index, place=place):
                    out[place] = ref[index]

                self.choose((requests, pool), refs, slot, store)

        return pl.pallas_call(
            kernel,
            in_specs=[SMEM, SMEM] + [VMEM] * len(arrays) + [ANY] * len(after),
            out_specs=VMEM,
            out_shape=jax.ShapeDtypeStruct(shape, arrays[0].dtype),
            compiler_params=params(4),
            cost_estimate=cost(0, 4 * int(np.prod(shape))),
            name="pick",
        )(*self.tables, *arrays, *after)


def base_products(tensor, own_tokens, other_tokens, query_weight, key_value_weight):
    half = own_tokens.shape[1]
    first = tensor == 0
    low = jnp.where(first, own_tokens, other_tokens)
    high = jnp.where(first, other_tokens, own_tokens)

    both = jnp.concatenate([low, high], axis=1)

    def product(weight):
        return jnp.dot(both, weight, preferred_element_type=jnp.float32)

    return jnp.concatenate([product(query_weight), product(key_value_weight)], axis=1)


def shrink_partial(routes, tokens, small_width):
    rows, half = tokens.shape
    rank = routes[0].parts[0].shape[1]
    counts = [len(route.arrays()) for route in routes]
    arrays = sum([route.arrays() for route in routes], [])

    def kernel(requests, pool, rows_ref, *refs):
        inputs, (out, small, maps) = refs[:-3], refs[-3:]
        at = 0
        for place, (route, count) in enumerate(zip(routes, counts)):

            def store(ref, index, place=place):
                maps[place * rank:(place + 1) * rank, :] = ref[index, :, :half]
                if place == 0:
                    small[...] = ref[index, :, half:]

            route.choose((requests, pool), inputs[at:at + count], 0, store)
            at += count
        out[...] = lax.dot_general(
            rows_ref[...], maps[...], (((1,), (1,)), ((), ())), preferred_element_type=jnp.float32)

    return pl.pallas_call(
        kernel,
        in_specs=[SMEM, SMEM] + [VMEM] * (1 + len(arrays)),
        out_specs=(VMEM, VMEM),
        out_shape=(
            jax.ShapeDtypeStruct((rows, rank * len(routes)), jnp.float32),
            jax.ShapeDtypeStruct((rank, small_width), tokens.dtype),
        ),
        scratch_shapes=[pltpu.VMEM((rank * len(routes), half), tokens.dtype)],
        compiler_params=params(6),
        cost_estimate=cost(2 * rows * half * rank * len(routes), 2 * rows * half),
        name="shrink",
    )(*routes[0].tables, tokens, *arrays)


def cut_parts(down_maps, small, rank):
    count, _, half = down_maps.shape
    width = sum(each.shape[2] for each in small)

    def kernel(down, *refs):
        small_refs, outs, sems = refs[:-4], refs[-4:-1], refs[-1]
        copies = [
            pltpu.make_async_copy(
                down.at[:, pl.ds(i * rank, rank), :], out.at[:, :, pl.ds(0, half)], sems.at[i])
            for i, out in enumerate(outs)
        ]
        at = half
        for i, each in enumerate(small_refs):
            more = each.shape[2]
            copies.append(pltpu.make_async_copy(each, outs[0].at[:, :, pl.ds(at, more)], sems.at[len(outs) + i]))
            at += more
        for copy in copies:
            copy.start()
        for copy in copies:
            copy.wait()

    return pl.pallas_call(
        kernel,
        in_specs=[ANY] * (1 + len(small)),
        out_specs=(VMEM,) * 3,
        out_shape=tuple(
            jax.ShapeDtypeStruct((count, rank, half + more), down_maps.dtype) for more in (width, 0, 0)),
        scratch_shapes=[pltpu.SemaphoreType.DMA((3 + len(small),))],
        compiler_params=params(4),
        cost_estimate=cost(0, 1 << 20),
        name="cut",
    )(down_maps, *small)


def rotary_tables(rows, width):
    half = width // 2
    freqs = np.float32(500000.0) ** (-(np.arange(half, dtype=np.float32) * np.float32(2.0) / np.float32(width)))
    angles = np.arange(rows, dtype=np.float32)[:, None] * freqs.astype(np.float32)[None, :]
    cosine, sine = np.cos(angles), np.sin(angles)
    return (
        np.concatenate([cosine, cosine], axis=1).astype(np.float32),
        np.concatenate([-sine, sine], axis=1).astype(np.float32),
    )


def attention_kernel(
    requests, pool, place, base_own, base_other, shrink_own, shrink_other, small_own, small_other, cosine, sine,
    weight_own, weight_other, *refs, query_columns, key_columns, route,
):
    out, up_map, tiles, sems = refs[-4:]
    tensor, length = place[0], place[1]

    def store(ref, index):
        up_map[...] = ref[index]

    route.choose((requests, pool), refs[:-4], 0, store)
    rank = small_own.shape[0]
    rows = base_own.shape[0]
    size = HEAD_SIZE
    shrink = (shrink_own[...] + shrink_other[...]).astype(jnp.bfloat16)
    first = tensor == 0

    def up(part, base, small, start, base_start, width):
        return base[:, base_start:base_start + width] + jnp.dot(
            part, small[:, start:start + width], preferred_element_type=jnp.float32)

    def rotate(v):
        return v * cosine[...] + pltpu.roll(v, size // 2, 1) * sine[...]

    own_side = shrink[:, rank:2 * rank], shrink[:, 2 * rank:3 * rank]
    own_part = jnp.where(first, own_side[0], own_side[1])
    other_part = jnp.where(first, own_side[1], own_side[0])
    own_kv = up(own_part, base_own, small_own, query_columns, query_columns, key_columns).astype(jnp.bfloat16)
    other_kv = up(other_part, base_other, small_other, query_columns, query_columns, key_columns).astype(jnp.bfloat16)
    keys = jnp.where(first, own_kv, other_kv)
    values = jnp.where(first, other_kv, own_kv)
    keys = rotate(keys.astype(jnp.float32)).astype(jnp.bfloat16)

    at = lax.broadcasted_iota(jnp.int32, (rows, rows), 0)
    to = lax.broadcasted_iota(jnp.int32, (rows, rows), 1)
    allowed = (to <= at) & (to < length)

    def heads(base, small):
        queries = up(shrink[:, :rank], base, small, 0, 0, query_columns)
        done = []
        for start in range(0, query_columns, size):
            query = rotate(queries[:, start:start + size]).astype(jnp.bfloat16)
            scores = lax.dot_general(
                query, keys, (((1,), (1,)), ((), ())), preferred_element_type=jnp.float32) * size ** (-0.5)
            scores = jnp.where(allowed, scores, -1e30)
            expo = jnp.exp(scores - jnp.max(scores, axis=1, keepdims=True))
            weights = (expo / jnp.sum(expo, axis=1, keepdims=True)).astype(jnp.bfloat16)
            done.append(jnp.dot(weights, values, preferred_element_type=jnp.float32).astype(jnp.bfloat16))
        return jnp.concatenate(done, axis=1)

    attended_own = heads(base_own, small_own)
    attended_other = heads(base_other, small_other)

    def down(attended, small):
        return lax.dot_general(
            attended, small[:, query_columns + key_columns:], (((1,), (1,)), ((), ())),
            preferred_element_type=jnp.float32)

    low = (down(attended_own, small_own) + down(attended_other, small_other)).astype(jnp.bfloat16)
    valid = lax.broadcasted_iota(jnp.int32, (rows, 1), 0) < length
    count, _, tile = tiles.shape
    copies = []
    for i in range(count):
        cut = slice(i * tile, (i + 1) * tile)
        own = jnp.dot(attended_own, weight_own[:, cut], preferred_element_type=jnp.float32)
        other = jnp.dot(attended_other, weight_other[:, cut], preferred_element_type=jnp.float32)
        base = own.astype(jnp.bfloat16).astype(jnp.float32) + other.astype(jnp.bfloat16).astype(jnp.float32)
        delta = jnp.dot(low, up_map[:, cut], preferred_element_type=jnp.float32)
        tiles[i] = jnp.where(valid, base + delta, 0.0).astype(tiles.dtype)
        copies.append(pltpu.make_async_copy(tiles.at[i], out.at[:, pl.ds(i * tile, tile)], sems.at[i]))
        copies[-1].start()
    for copy in copies:
        copy.wait()


def attention(route, place, base, shrink, small, weight, query_columns, key_columns):
    rows = base[0].shape[0]
    columns = weight[0].shape[1]
    cosine, sine = rotary_tables(rows, HEAD_SIZE)
    arrays = route.arrays()
    operands = (*base, *shrink, *small, cosine, sine, *weight, *arrays)
    tile = 512
    return pl.pallas_call(
        functools.partial(attention_kernel, query_columns=query_columns, key_columns=key_columns, route=route),
        in_specs=[SMEM] * 3 + [VMEM] * len(operands),
        out_specs=ANY,
        out_shape=jax.ShapeDtypeStruct((rows, columns), arrays[0].dtype),
        scratch_shapes=[
            pltpu.VMEM(arrays[0].shape[1:], arrays[0].dtype),
            pltpu.VMEM((columns // tile, rows, tile), arrays[0].dtype),
            pltpu.SemaphoreType.DMA((columns // tile,)),
        ],
        compiler_params=params(8),
        cost_estimate=cost(4 * rows * query_columns * columns, 4 * query_columns * columns),
        name="attention",
    )(*route.tables, place, *operands)


def orders(bits):
    each = list(range(bits))
    first = each
    second = [1, 0] + each[2:] if bits > 1 else each
    third = [each[-1]] + each[:-1]
    return first, second, third


def local(
    devices,
    tokens,
    query_weight,
    key_value_weight,
    output_weight,
    adapter_down_maps,
    adapter_query_up,
    adapter_key_value_up,
    adapter_output_down,
    adapter_output_up,
    request_adapter,
    adapter_pool_row,
    lengths,
):
    tensor = lax.axis_index("tensor")
    pair = [(0, 1), (1, 0)]
    half = tokens.shape[1]
    rank = adapter_query_up.shape[1]
    query_columns = query_weight.shape[1]
    key_columns = key_value_weight.shape[1]
    place = jnp.stack([tensor, lengths[0]]).astype(jnp.int32)

    def swap(x):
        return lax.ppermute(x, "tensor", pair)

    small = (adapter_query_up, adapter_key_value_up, adapter_output_down)
    small_width = sum(each.shape[2] for each in small)
    first, second, third = orders(devices.bit_length() - 1)

    def route(part, order):
        return Route(part, order, devices, request_adapter, adapter_pool_row)

    parts = cut_parts(adapter_down_maps, small, rank)
    first_route, second_route, third_route = (
        route(part, order) for part, order in zip(parts, (first, second, third)))
    routes = [first_route, second_route, third_route]
    up_route = route(adapter_output_up, first)
    weight_other = swap(output_weight)
    other_tokens = swap(tokens)
    for each in (third_route, second_route, first_route, up_route):
        each.step()
    base_own = base_products(tensor, tokens, other_tokens, query_weight, key_value_weight)
    base_other = swap(base_own)
    weight_near, weight_far = (
        lax.dynamic_slice_in_dim(weight, tensor * half, half, 1) for weight in (output_weight, weight_other))
    last = (base_own,)
    turns = (first_route, second_route, third_route, up_route, first_route, second_route, third_route, up_route) * 1
    for turn, each in enumerate(turns):
        if turn == 3:
            last += (weight_near, weight_far)
        sent = each.step(last)
        last = (each.arrays()[-1] if sent is None else sent,)

    shrink_own, small_own = shrink_partial(routes, tokens, small_width)
    return attention(
        up_route, place, (base_own, base_other), (shrink_own, swap(shrink_own)), (small_own, swap(small_own)),
        (weight_near, weight_far), query_columns, key_columns)


def solution(mesh):
    placed = (
        P(("group", "serve"), "tensor"),
        P(None, "tensor"),
        P(None, "tensor"),
        P("tensor", None),
        P(("group", "serve"), None, "tensor"),
        P(("group", "serve"), None, "tensor"),
        P(("group", "serve"), None, "tensor"),
        P(("group", "serve"), None, "tensor"),
        P(("group", "serve"), None, "tensor"),
        P("group"),
        P("group"),
        P(("group", "serve")),
    )
    return jax.shard_map(
        functools.partial(local, mesh.shape["serve"]),
        mesh=mesh,
        in_specs=placed,
        out_specs=P(("group", "serve"), "tensor"),
        check_vma=False,
    )
```

```python
import functools

import jax
import jax.numpy as jnp
import numpy as np
from jax import lax
from jax.experimental import pallas as pl
from jax.experimental.pallas import tpu as pltpu
from jax.sharding import PartitionSpec as P

HEAD_SIZE = 128
MIB = 1 << 20
VMEM = pl.BlockSpec(memory_space=pltpu.VMEM)
SMEM = pl.BlockSpec(memory_space=pltpu.SMEM)
ANY = pl.BlockSpec(memory_space=pl.ANY)


def span(bits):
    masks = [0]
    for bit in bits:
        masks += [mask ^ bit for mask in masks]
    return masks


def params(mib):
    return pltpu.CompilerParams(vmem_limit_bytes=mib * MIB)


def cost(flops, bytes_accessed):
    return pl.CostEstimate(flops=flops, transcendentals=0, bytes_accessed=bytes_accessed)


class Route:
    def __init__(self, part, order, devices, request_adapter, adapter_pool_row):
        self.parts, self.masks = [part], [0]
        self.packets, self.known = [], []
        self.bits = [1 << bit for bit in order]
        self.done = 0
        self.devices = devices
        self.tables = (request_adapter, adapter_pool_row)
        self.held = part.shape[0]

    def arrays(self):
        return self.parts + self.packets

    def choose(self, tables, refs, slot, store):
        requests, pool = tables
        here = lax.axis_index("serve")
        wanted = pool[requests[here ^ slot]]
        offset = (wanted // self.held) ^ here
        for ref, mask in zip(refs, self.masks):

            @pl.when(offset == mask)
            def _(ref=ref):
                store(ref, wanted % self.held)

        for ref, (masks, slots) in zip(refs[len(self.masks):], self.known):
            arrived = functools.reduce(lambda a, b: a | b, [offset == mask for mask in masks])

            @pl.when(arrived)
            def _(ref=ref, slots=slots):
                store(ref, slots.index(slot))

    def step(self, after=()):
        bit = self.bits[self.done]
        slots = span(self.bits[self.done + 1:])
        pairs = [(i, i ^ bit) for i in range(self.devices)]
        out = None
        if not self.known and self.held * len(self.parts) <= len(slots):
            self.parts += [lax.ppermute(part, "serve", pairs) for part in self.parts]
            self.masks += [mask ^ bit for mask in self.masks]
        else:
            out = self.pick([bit ^ slot for slot in slots], after)
            self.packets.append(lax.ppermute(out, "serve", pairs))
            self.known.append(([bit ^ mask for mask in span(self.bits[:self.done])], slots))
        self.done += 1
        return out

    def pick(self, slots, after):
        arrays = self.arrays()
        shape = (len(slots),) + arrays[0].shape[1:]

        def kernel(requests, pool, *refs):
            out = refs[-1]
            for place, slot in enumerate(slots):
                out[place] = refs[0][0]

                def store(ref, index, place=place):
                    out[place] = ref[index]

                self.choose((requests, pool), refs, slot, store)

        return pl.pallas_call(
            kernel,
            in_specs=[SMEM, SMEM] + [VMEM] * len(arrays) + [ANY] * len(after),
            out_specs=VMEM,
            out_shape=jax.ShapeDtypeStruct(shape, arrays[0].dtype),
            compiler_params=params(4),
            cost_estimate=cost(0, 4 * int(np.prod(shape))),
            name="pick",
        )(*self.tables, *arrays, *after)


def base_products(tensor, own_tokens, other_tokens, query_weight, key_value_weight):
    half = own_tokens.shape[1]
    first = tensor == 0
    low = jnp.where(first, own_tokens, other_tokens)
    high = jnp.where(first, other_tokens, own_tokens)

    both = jnp.concatenate([low, high], axis=1)

    def product(weight):
        return jnp.dot(both, weight, preferred_element_type=jnp.float32)

    return jnp.concatenate([product(query_weight), product(key_value_weight)], axis=1)


def shrink_partial(routes, tokens, small_width):
    rows, half = tokens.shape
    rank = routes[0].parts[0].shape[1]
    counts = [len(route.arrays()) for route in routes]
    arrays = sum([route.arrays() for route in routes], [])

    def kernel(requests, pool, rows_ref, *refs):
        inputs, (out, small, maps) = refs[:-3], refs[-3:]
        at = 0
        for place, (route, count) in enumerate(zip(routes, counts)):

            def store(ref, index, place=place):
                maps[place * rank:(place + 1) * rank, :] = ref[index, :, :half]
                if place == 0:
                    small[...] = ref[index, :, half:]

            route.choose((requests, pool), inputs[at:at + count], 0, store)
            at += count
        out[...] = lax.dot_general(
            rows_ref[...], maps[...], (((1,), (1,)), ((), ())), preferred_element_type=jnp.float32)

    return pl.pallas_call(
        kernel,
        in_specs=[SMEM, SMEM] + [VMEM] * (1 + len(arrays)),
        out_specs=(VMEM, VMEM),
        out_shape=(
            jax.ShapeDtypeStruct((rows, rank * len(routes)), jnp.float32),
            jax.ShapeDtypeStruct((rank, small_width), tokens.dtype),
        ),
        scratch_shapes=[pltpu.VMEM((rank * len(routes), half), tokens.dtype)],
        compiler_params=params(6),
        cost_estimate=cost(2 * rows * half * rank * len(routes), 2 * rows * half),
        name="shrink",
    )(*routes[0].tables, tokens, *arrays)


def rotary_tables(rows, width):
    half = width // 2
    freqs = np.float32(500000.0) ** (-(np.arange(half, dtype=np.float32) * np.float32(2.0) / np.float32(width)))
    angles = np.arange(rows, dtype=np.float32)[:, None] * freqs.astype(np.float32)[None, :]
    cosine, sine = np.cos(angles), np.sin(angles)
    return (
        np.concatenate([cosine, cosine], axis=1).astype(np.float32),
        np.concatenate([-sine, sine], axis=1).astype(np.float32),
    )


def attention_kernel(
    requests, pool, place, base_own, base_other, shrink_own, shrink_other, small_own, small_other, cosine, sine,
    weight_own, weight_other, *refs, query_columns, key_columns, route,
):
    out, up_map, tiles, sems = refs[-4:]
    tensor, length = place[0], place[1]

    def store(ref, index):
        up_map[...] = ref[index]

    route.choose((requests, pool), refs[:-4], 0, store)
    rank = small_own.shape[0]
    rows = base_own.shape[0]
    size = HEAD_SIZE
    shrink = (shrink_own[...] + shrink_other[...]).astype(jnp.bfloat16)
    first = tensor == 0

    def up(part, base, small, start, base_start, width):
        return base[:, base_start:base_start + width] + jnp.dot(
            part, small[:, start:start + width], preferred_element_type=jnp.float32)

    def rotate(v):
        return v * cosine[...] + pltpu.roll(v, size // 2, 1) * sine[...]

    own_side = shrink[:, rank:2 * rank], shrink[:, 2 * rank:3 * rank]
    own_part = jnp.where(first, own_side[0], own_side[1])
    other_part = jnp.where(first, own_side[1], own_side[0])
    own_kv = up(own_part, base_own, small_own, query_columns, query_columns, key_columns).astype(jnp.bfloat16)
    other_kv = up(other_part, base_other, small_other, query_columns, query_columns, key_columns).astype(jnp.bfloat16)
    keys = jnp.where(first, own_kv, other_kv)
    values = jnp.where(first, other_kv, own_kv)
    keys = rotate(keys.astype(jnp.float32)).astype(jnp.bfloat16)

    at = lax.broadcasted_iota(jnp.int32, (rows, rows), 0)
    to = lax.broadcasted_iota(jnp.int32, (rows, rows), 1)
    allowed = (to <= at) & (to < length)

    def heads(base, small):
        queries = up(shrink[:, :rank], base, small, 0, 0, query_columns)
        done = []
        for start in range(0, query_columns, size):
            query = rotate(queries[:, start:start + size]).astype(jnp.bfloat16)
            scores = lax.dot_general(
                query, keys, (((1,), (1,)), ((), ())), preferred_element_type=jnp.float32) * size ** (-0.5)
            scores = jnp.where(allowed, scores, -1e30)
            expo = jnp.exp(scores - jnp.max(scores, axis=1, keepdims=True))
            weights = (expo / jnp.sum(expo, axis=1, keepdims=True)).astype(jnp.bfloat16)
            done.append(jnp.dot(weights, values, preferred_element_type=jnp.float32).astype(jnp.bfloat16))
        return jnp.concatenate(done, axis=1)

    attended_own = heads(base_own, small_own)
    attended_other = heads(base_other, small_other)

    def down(attended, small):
        return lax.dot_general(
            attended, small[:, query_columns + key_columns:], (((1,), (1,)), ((), ())),
            preferred_element_type=jnp.float32)

    low = (down(attended_own, small_own) + down(attended_other, small_other)).astype(jnp.bfloat16)
    valid = lax.broadcasted_iota(jnp.int32, (rows, 1), 0) < length
    count, _, tile = tiles.shape
    copies = []
    for i in range(count):
        cut = slice(i * tile, (i + 1) * tile)
        own = jnp.dot(attended_own, weight_own[:, cut], preferred_element_type=jnp.float32)
        other = jnp.dot(attended_other, weight_other[:, cut], preferred_element_type=jnp.float32)
        base = own.astype(jnp.bfloat16).astype(jnp.float32) + other.astype(jnp.bfloat16).astype(jnp.float32)
        delta = jnp.dot(low, up_map[:, cut], preferred_element_type=jnp.float32)
        tiles[i] = jnp.where(valid, base + delta, 0.0).astype(tiles.dtype)
        copies.append(pltpu.make_async_copy(tiles.at[i], out.at[:, pl.ds(i * tile, tile)], sems.at[i]))
        copies[-1].start()
    for copy in copies:
        copy.wait()


def attention(route, place, base, shrink, small, weight, query_columns, key_columns):
    rows = base[0].shape[0]
    columns = weight[0].shape[1]
    cosine, sine = rotary_tables(rows, HEAD_SIZE)
    arrays = route.arrays()
    operands = (*base, *shrink, *small, cosine, sine, *weight, *arrays)
    tile = 512
    return pl.pallas_call(
        functools.partial(attention_kernel, query_columns=query_columns, key_columns=key_columns, route=route),
        in_specs=[SMEM] * 3 + [VMEM] * len(operands),
        out_specs=ANY,
        out_shape=jax.ShapeDtypeStruct((rows, columns), arrays[0].dtype),
        scratch_shapes=[
            pltpu.VMEM(arrays[0].shape[1:], arrays[0].dtype),
            pltpu.VMEM((columns // tile, rows, tile), arrays[0].dtype),
            pltpu.SemaphoreType.DMA((columns // tile,)),
        ],
        compiler_params=params(8),
        cost_estimate=cost(4 * rows * query_columns * columns, 4 * query_columns * columns),
        name="attention",
    )(*route.tables, place, *operands)


def orders(bits):
    each = list(range(bits))
    first = each
    second = [1, 0] + each[2:] if bits > 1 else each
    third = [each[-1]] + each[:-1]
    return first, second, third


def local(
    devices,
    tokens,
    query_weight,
    key_value_weight,
    output_weight,
    adapter_down_maps,
    adapter_query_up,
    adapter_key_value_up,
    adapter_output_down,
    adapter_output_up,
    request_adapter,
    adapter_pool_row,
    lengths,
):
    tensor = lax.axis_index("tensor")
    pair = [(0, 1), (1, 0)]
    half = tokens.shape[1]
    rank = adapter_query_up.shape[1]
    query_columns = query_weight.shape[1]
    key_columns = key_value_weight.shape[1]
    place = jnp.stack([tensor, lengths[0]]).astype(jnp.int32)

    def swap(x):
        return lax.ppermute(x, "tensor", pair)

    small = (adapter_query_up, adapter_key_value_up, adapter_output_down)
    small_width = sum(each.shape[2] for each in small)
    first, second, third = orders(devices.bit_length() - 1)

    def route(part, order):
        return Route(part, order, devices, request_adapter, adapter_pool_row)

    down = [adapter_down_maps[:, i * rank:(i + 1) * rank] for i in range(3)]
    parts = (jnp.concatenate([down[0], *small], axis=2), down[1], down[2])
    first_route, second_route, third_route = (
        route(part, order) for part, order in zip(parts, (first, second, third)))
    routes = [first_route, second_route, third_route]
    up_route = route(adapter_output_up, first)
    weight_other = swap(output_weight)
    other_tokens = swap(tokens)
    for each in (third_route, second_route, first_route, up_route):
        each.step()
    base_own = base_products(tensor, tokens, other_tokens, query_weight, key_value_weight)
    base_other = swap(base_own)
    weight_near, weight_far = (
        lax.dynamic_slice_in_dim(weight, tensor * half, half, 1) for weight in (output_weight, weight_other))
    last = (base_own,)
    turns = (first_route, second_route, third_route, up_route, first_route, second_route, third_route, up_route) * 1
    for turn, each in enumerate(turns):
        if turn == 3:
            last += (weight_near, weight_far)
        sent = each.step(last)
        last = (each.arrays()[-1] if sent is None else sent,)

    shrink_own, small_own = shrink_partial(routes, tokens, small_width)
    return attention(
        up_route, place, (base_own, base_other), (shrink_own, swap(shrink_own)), (small_own, swap(small_own)),
        (weight_near, weight_far), query_columns, key_columns)


def solution(mesh):
    placed = (
        P(("group", "serve"), "tensor"),
        P(None, "tensor"),
        P(None, "tensor"),
        P("tensor", None),
        P(("group", "serve"), None, "tensor"),
        P(("group", "serve"), None, "tensor"),
        P(("group", "serve"), None, "tensor"),
        P(("group", "serve"), None, "tensor"),
        P(("group", "serve"), None, "tensor"),
        P("group"),
        P("group"),
        P(("group", "serve")),
    )
    return jax.shard_map(
        functools.partial(local, mesh.shape["serve"]),
        mesh=mesh,
        in_specs=placed,
        out_specs=P(("group", "serve"), "tensor"),
        check_vma=False,
    )
```

```python
import functools

import jax
import jax.numpy as jnp
import numpy as np
from jax import lax
from jax.experimental import pallas as pl
from jax.experimental.pallas import tpu as pltpu
from jax.sharding import PartitionSpec as P

HEAD_SIZE = 128
MIB = 1 << 20
VMEM = pl.BlockSpec(memory_space=pltpu.VMEM)
SMEM = pl.BlockSpec(memory_space=pltpu.SMEM)
ANY = pl.BlockSpec(memory_space=pl.ANY)


def span(bits):
    masks = [0]
    for bit in bits:
        masks += [mask ^ bit for mask in masks]
    return masks


def params(mib):
    return pltpu.CompilerParams(vmem_limit_bytes=mib * MIB)


def cost(flops, bytes_accessed):
    return pl.CostEstimate(flops=flops, transcendentals=0, bytes_accessed=bytes_accessed)


class Route:
    def __init__(self, part, order, devices, request_adapter, adapter_pool_row):
        self.parts, self.masks = [part], [0]
        self.packets, self.known = [], []
        self.bits = [1 << bit for bit in order]
        self.done = 0
        self.devices = devices
        self.tables = (request_adapter, adapter_pool_row)
        self.held = part.shape[0]

    def arrays(self):
        return self.parts + self.packets

    def choose(self, tables, refs, slot, store):
        requests, pool = tables
        here = lax.axis_index("serve")
        wanted = pool[requests[here ^ slot]]
        offset = (wanted // self.held) ^ here
        for ref, mask in zip(refs, self.masks):

            @pl.when(offset == mask)
            def _(ref=ref):
                store(ref, wanted % self.held)

        for ref, (masks, slots) in zip(refs[len(self.masks):], self.known):
            arrived = functools.reduce(lambda a, b: a | b, [offset == mask for mask in masks])

            @pl.when(arrived)
            def _(ref=ref, slots=slots):
                store(ref, slots.index(slot))

    def step(self, after=()):
        bit = self.bits[self.done]
        slots = span(self.bits[self.done + 1:])
        pairs = [(i, i ^ bit) for i in range(self.devices)]
        out = None
        if not self.known and self.held * len(self.parts) <= len(slots):
            self.parts += [lax.ppermute(part, "serve", pairs) for part in self.parts]
            self.masks += [mask ^ bit for mask in self.masks]
        else:
            out = self.pick([bit ^ slot for slot in slots], after)
            self.packets.append(lax.ppermute(out, "serve", pairs))
            self.known.append(([bit ^ mask for mask in span(self.bits[:self.done])], slots))
        self.done += 1
        return out

    def pick(self, slots, after):
        arrays = self.arrays()
        shape = (len(slots),) + arrays[0].shape[1:]

        def kernel(requests, pool, *refs):
            out = refs[-1]
            for place, slot in enumerate(slots):
                out[place] = refs[0][0]

                def store(ref, index, place=place):
                    out[place] = ref[index]

                self.choose((requests, pool), refs, slot, store)

        return pl.pallas_call(
            kernel,
            in_specs=[SMEM, SMEM] + [VMEM] * len(arrays) + [ANY] * len(after),
            out_specs=VMEM,
            out_shape=jax.ShapeDtypeStruct(shape, arrays[0].dtype),
            compiler_params=params(4),
            cost_estimate=cost(0, 4 * int(np.prod(shape))),
            name="pick",
        )(*self.tables, *arrays, *after)


def base_products(tensor, own_tokens, other_tokens, query_weight, key_value_weight):
    half = own_tokens.shape[1]
    first = tensor == 0
    low = jnp.where(first, own_tokens, other_tokens)
    high = jnp.where(first, other_tokens, own_tokens)

    both = jnp.concatenate([low, high], axis=1)

    def product(weight):
        return jnp.dot(both, weight, preferred_element_type=jnp.float32)

    return jnp.concatenate([product(query_weight), product(key_value_weight)], axis=1)


def shrink_partial(routes, tokens, small_width, after):
    rows, half = tokens.shape
    rank = routes[0].parts[0].shape[1]
    counts = [len(route.arrays()) for route in routes]
    arrays = sum([route.arrays() for route in routes], [])

    def kernel(requests, pool, rows_ref, *refs):
        inputs, (out, small, maps) = refs[:-3], refs[-3:]
        at = 0
        for place, (route, count) in enumerate(zip(routes, counts)):

            def store(ref, index, place=place):
                maps[place * rank:(place + 1) * rank, :] = ref[index, :, :half]
                if place == 0:
                    small[...] = ref[index, :, half:]

            route.choose((requests, pool), inputs[at:at + count], 0, store)
            at += count
        out[...] = lax.dot_general(
            rows_ref[...], maps[...], (((1,), (1,)), ((), ())), preferred_element_type=jnp.float32)

    return pl.pallas_call(
        kernel,
        in_specs=[SMEM, SMEM] + [VMEM] * (1 + len(arrays)) + [ANY] * len(after),
        out_specs=(VMEM, VMEM),
        out_shape=(
            jax.ShapeDtypeStruct((rows, rank * len(routes)), jnp.float32),
            jax.ShapeDtypeStruct((rank, small_width), tokens.dtype),
        ),
        scratch_shapes=[pltpu.VMEM((rank * len(routes), half), tokens.dtype)],
        compiler_params=params(6),
        cost_estimate=cost(2 * rows * half * rank * len(routes), 2 * rows * half),
        name="shrink",
    )(*routes[0].tables, tokens, *arrays, *after)


def rotary_tables(rows, width):
    half = width // 2
    freqs = np.float32(500000.0) ** (-(np.arange(half, dtype=np.float32) * np.float32(2.0) / np.float32(width)))
    angles = np.arange(rows, dtype=np.float32)[:, None] * freqs.astype(np.float32)[None, :]
    cosine, sine = np.cos(angles), np.sin(angles)
    return (
        np.concatenate([cosine, cosine], axis=1).astype(np.float32),
        np.concatenate([-sine, sine], axis=1).astype(np.float32),
    )


def attention_kernel(
    place, base_own, base_other, shrink_own, shrink_other, small_own, small_other, cosine, sine,
    weight_own, weight_other, out, low_out, *, query_columns, key_columns,
):
    tensor, length = place[0], place[1]
    rank = small_own.shape[0]
    rows = base_own.shape[0]
    size = HEAD_SIZE
    shrink = (shrink_own[...] + shrink_other[...]).astype(jnp.bfloat16)
    first = tensor == 0

    def up(part, base, small, start, base_start, width):
        return base[:, base_start:base_start + width] + jnp.dot(
            part, small[:, start:start + width], preferred_element_type=jnp.float32)

    def rotate(v):
        return v * cosine[...] + pltpu.roll(v, size // 2, 1) * sine[...]

    own_side = shrink[:, rank:2 * rank], shrink[:, 2 * rank:3 * rank]
    own_part = jnp.where(first, own_side[0], own_side[1])
    other_part = jnp.where(first, own_side[1], own_side[0])
    own_kv = up(own_part, base_own, small_own, query_columns, query_columns, key_columns).astype(jnp.bfloat16)
    other_kv = up(other_part, base_other, small_other, query_columns, query_columns, key_columns).astype(jnp.bfloat16)
    keys = jnp.where(first, own_kv, other_kv)
    values = jnp.where(first, other_kv, own_kv)
    keys = rotate(keys.astype(jnp.float32)).astype(jnp.bfloat16)

    at = lax.broadcasted_iota(jnp.int32, (rows, rows), 0)
    to = lax.broadcasted_iota(jnp.int32, (rows, rows), 1)
    allowed = (to <= at) & (to < length)

    def heads(base, small):
        queries = up(shrink[:, :rank], base, small, 0, 0, query_columns)
        done = []
        for start in range(0, query_columns, size):
            query = rotate(queries[:, start:start + size]).astype(jnp.bfloat16)
            scores = lax.dot_general(
                query, keys, (((1,), (1,)), ((), ())), preferred_element_type=jnp.float32) * size ** (-0.5)
            scores = jnp.where(allowed, scores, -1e30)
            expo = jnp.exp(scores - jnp.max(scores, axis=1, keepdims=True))
            weights = (expo / jnp.sum(expo, axis=1, keepdims=True)).astype(jnp.bfloat16)
            done.append(jnp.dot(weights, values, preferred_element_type=jnp.float32).astype(jnp.bfloat16))
        return jnp.concatenate(done, axis=1)

    attended_own = heads(base_own, small_own)
    attended_other = heads(base_other, small_other)

    def down(attended, small):
        return lax.dot_general(
            attended, small[:, query_columns + key_columns:], (((1,), (1,)), ((), ())),
            preferred_element_type=jnp.float32)

    low_out[...] = (down(attended_own, small_own) + down(attended_other, small_other)).astype(jnp.bfloat16)
    tile = 512
    for start in range(0, out.shape[1], tile):
        cut = slice(start, start + tile)
        own = jnp.dot(attended_own, weight_own[:, cut], preferred_element_type=jnp.float32)
        other = jnp.dot(attended_other, weight_other[:, cut], preferred_element_type=jnp.float32)
        out[:, cut] = own.astype(jnp.bfloat16).astype(jnp.float32) + other.astype(jnp.bfloat16).astype(jnp.float32)


def attention(place, base, shrink, small, weight, query_columns, key_columns):
    rows = base[0].shape[0]
    columns = weight[0].shape[1]
    cosine, sine = rotary_tables(rows, HEAD_SIZE)
    operands = (*base, *shrink, *small, cosine, sine, *weight)
    return pl.pallas_call(
        functools.partial(attention_kernel, query_columns=query_columns, key_columns=key_columns),
        in_specs=[SMEM] + [VMEM] * len(operands),
        out_specs=(VMEM, VMEM),
        out_shape=(
            jax.ShapeDtypeStruct((rows, columns), jnp.float32),
            jax.ShapeDtypeStruct((rows, small[0].shape[0]), jnp.bfloat16),
        ),
        compiler_params=params(8),
        cost_estimate=cost(4 * rows * query_columns * columns, 4 * query_columns * columns),
        name="attention",
    )(place, *operands)


def finish(route, place, base, low):
    rows, columns = base.shape
    arrays = route.arrays()
    tile = 512

    def kernel(requests, pool, place, base_ref, low_ref, *refs):
        out, up_map, tiles, sems = refs[-4:]

        def store(ref, index):
            up_map[...] = ref[index]

        route.choose((requests, pool), refs[:-4], 0, store)
        valid = lax.broadcasted_iota(jnp.int32, (rows, 1), 0) < place[1]
        copies = []
        for i in range(columns // tile):
            cut = slice(i * tile, (i + 1) * tile)
            delta = jnp.dot(low_ref[...], up_map[:, cut], preferred_element_type=jnp.float32)
            tiles[i] = jnp.where(valid, base_ref[:, cut] + delta, 0.0).astype(tiles.dtype)
            copies.append(pltpu.make_async_copy(tiles.at[i], out.at[:, pl.ds(i * tile, tile)], sems.at[i]))
            copies[-1].start()
        for copy in copies:
            copy.wait()

    return pl.pallas_call(
        kernel,
        in_specs=[SMEM] * 3 + [VMEM] * (2 + len(arrays)),
        out_specs=ANY,
        out_shape=jax.ShapeDtypeStruct((rows, columns), arrays[0].dtype),
        scratch_shapes=[
            pltpu.VMEM(arrays[0].shape[1:], arrays[0].dtype),
            pltpu.VMEM((columns // tile, rows, tile), arrays[0].dtype),
            pltpu.SemaphoreType.DMA((columns // tile,)),
        ],
        compiler_params=params(8),
        cost_estimate=cost(2 * rows * low.shape[1] * columns, 6 * rows * columns),
        name="finish",
    )(*route.tables, place, base, low, *arrays)


def orders(bits):
    each = list(range(bits))
    first = each
    second = [1, 0] + each[2:] if bits > 1 else each
    third = [each[-1]] + each[:-1]
    return first, second, third


def local(
    devices,
    tokens,
    query_weight,
    key_value_weight,
    output_weight,
    adapter_down_maps,
    adapter_query_up,
    adapter_key_value_up,
    adapter_output_down,
    adapter_output_up,
    request_adapter,
    adapter_pool_row,
    lengths,
):
    tensor = lax.axis_index("tensor")
    pair = [(0, 1), (1, 0)]
    half = tokens.shape[1]
    rank = adapter_query_up.shape[1]
    query_columns = query_weight.shape[1]
    key_columns = key_value_weight.shape[1]
    place = jnp.stack([tensor, lengths[0]]).astype(jnp.int32)

    def swap(x):
        return lax.ppermute(x, "tensor", pair)

    small = (adapter_query_up, adapter_key_value_up, adapter_output_down)
    small_width = sum(each.shape[2] for each in small)
    first, second, third = orders(devices.bit_length() - 1)

    def route(part, order):
        return Route(part, order, devices, request_adapter, adapter_pool_row)

    down = [adapter_down_maps[:, i * rank:(i + 1) * rank] for i in range(3)]
    parts = (jnp.concatenate([down[0], *small], axis=2), down[1], down[2])
    first_route, second_route, third_route = (
        route(part, order) for part, order in zip(parts, (first, second, third)))
    routes = [first_route, second_route, third_route]
    up_route = route(adapter_output_up, first)
    weight_other = swap(output_weight)
    other_tokens = swap(tokens)
    for each in (third_route, second_route, first_route, up_route):
        each.step()
    base_own = base_products(tensor, tokens, other_tokens, query_weight, key_value_weight)
    base_other = swap(base_own)
    weight_near, weight_far = (
        lax.dynamic_slice_in_dim(weight, tensor * half, half, 1) for weight in (output_weight, weight_other))
    last = (base_own,)
    turns = (first_route, second_route, third_route, up_route, first_route, second_route, third_route, up_route) * 1
    for turn, each in enumerate(turns):
        if turn == 3:
            last += (weight_near, weight_far)
        sent = each.step(last)
        last = (each.arrays()[-1] if sent is None else sent,)

    shrink_own, small_own = shrink_partial(routes, tokens, small_width, last)
    base, low = attention(
        place, (base_own, base_other), (shrink_own, swap(shrink_own)), (small_own, swap(small_own)),
        (weight_near, weight_far), query_columns, key_columns)
    return finish(up_route, place, base, low)


def solution(mesh):
    placed = (
        P(("group", "serve"), "tensor"),
        P(None, "tensor"),
        P(None, "tensor"),
        P("tensor", None),
        P(("group", "serve"), None, "tensor"),
        P(("group", "serve"), None, "tensor"),
        P(("group", "serve"), None, "tensor"),
        P(("group", "serve"), None, "tensor"),
        P(("group", "serve"), None, "tensor"),
        P("group"),
        P("group"),
        P(("group", "serve")),
    )
    return jax.shard_map(
        functools.partial(local, mesh.shape["serve"]),
        mesh=mesh,
        in_specs=placed,
        out_specs=P(("group", "serve"), "tensor"),
        check_vma=False,
    )
```

```python
import functools

import jax
import jax.numpy as jnp
import numpy as np
from jax import lax
from jax.experimental import pallas as pl
from jax.experimental.pallas import tpu as pltpu
from jax.sharding import PartitionSpec as P

HEAD_SIZE = 128
MIB = 1 << 20
VMEM = pl.BlockSpec(memory_space=pltpu.VMEM)
SMEM = pl.BlockSpec(memory_space=pltpu.SMEM)
ANY = pl.BlockSpec(memory_space=pl.ANY)


def span(bits):
    masks = [0]
    for bit in bits:
        masks += [mask ^ bit for mask in masks]
    return masks


def params(mib):
    return pltpu.CompilerParams(vmem_limit_bytes=mib * MIB)


def cost(flops, bytes_accessed):
    return pl.CostEstimate(flops=flops, transcendentals=0, bytes_accessed=bytes_accessed)


class Route:
    def __init__(self, part, order, devices, request_adapter, adapter_pool_row):
        self.parts, self.masks = [part], [0]
        self.packets, self.known = [], []
        self.bits = [1 << bit for bit in order]
        self.done = 0
        self.devices = devices
        self.tables = (request_adapter, adapter_pool_row)
        self.held = part.shape[0]

    def arrays(self):
        return self.parts + self.packets

    def choose(self, tables, refs, slot, store):
        requests, pool = tables
        here = lax.axis_index("serve")
        wanted = pool[requests[here ^ slot]]
        offset = (wanted // self.held) ^ here
        for ref, mask in zip(refs, self.masks):

            @pl.when(offset == mask)
            def _(ref=ref):
                store(ref, wanted % self.held)

        for ref, (masks, slots) in zip(refs[len(self.masks):], self.known):
            arrived = functools.reduce(lambda a, b: a | b, [offset == mask for mask in masks])

            @pl.when(arrived)
            def _(ref=ref, slots=slots):
                store(ref, slots.index(slot))

    def step(self, after=()):
        bit = self.bits[self.done]
        slots = span(self.bits[self.done + 1:])
        pairs = [(i, i ^ bit) for i in range(self.devices)]
        out = None
        if not self.known and self.held * len(self.parts) <= len(slots):
            self.parts += [lax.ppermute(part, "serve", pairs) for part in self.parts]
            self.masks += [mask ^ bit for mask in self.masks]
        else:
            out = self.pick([bit ^ slot for slot in slots], after)
            self.packets.append(lax.ppermute(out, "serve", pairs))
            self.known.append(([bit ^ mask for mask in span(self.bits[:self.done])], slots))
        self.done += 1
        return out

    def pick(self, slots, after):
        arrays = self.arrays()
        shape = (len(slots),) + arrays[0].shape[1:]

        def kernel(requests, pool, *refs):
            out = refs[-1]
            for place, slot in enumerate(slots):
                out[place] = refs[0][0]

                def store(ref, index, place=place):
                    out[place] = ref[index]

                self.choose((requests, pool), refs, slot, store)

        return pl.pallas_call(
            kernel,
            in_specs=[SMEM, SMEM] + [VMEM] * len(arrays) + [ANY] * len(after),
            out_specs=VMEM,
            out_shape=jax.ShapeDtypeStruct(shape, arrays[0].dtype),
            compiler_params=params(4),
            cost_estimate=cost(0, 4 * int(np.prod(shape))),
            name="pick",
        )(*self.tables, *arrays, *after)


def base_products(tensor, own_tokens, other_tokens, query_weight, key_value_weight):
    half = own_tokens.shape[1]
    first = tensor == 0
    low = jnp.where(first, own_tokens, other_tokens)
    high = jnp.where(first, other_tokens, own_tokens)

    both = jnp.concatenate([low, high], axis=1)

    def product(weight):
        return jnp.dot(both, weight, preferred_element_type=jnp.float32)

    return jnp.concatenate([product(query_weight), product(key_value_weight)], axis=1)


def shrink_partial(routes, tokens, small_width, after):
    rows, half = tokens.shape
    rank = routes[0].parts[0].shape[1]
    counts = [len(route.arrays()) for route in routes]
    arrays = sum([route.arrays() for route in routes], [])

    def kernel(requests, pool, rows_ref, *refs):
        inputs, (out, small, maps) = refs[:-3], refs[-3:]
        at = 0
        for place, (route, count) in enumerate(zip(routes, counts)):

            def store(ref, index, place=place):
                maps[place * rank:(place + 1) * rank, :] = ref[index, :, :half]
                if place == 0:
                    small[...] = ref[index, :, half:]

            route.choose((requests, pool), inputs[at:at + count], 0, store)
            at += count
        out[...] = lax.dot_general(
            rows_ref[...], maps[...], (((1,), (1,)), ((), ())), preferred_element_type=jnp.float32)

    return pl.pallas_call(
        kernel,
        in_specs=[SMEM, SMEM] + [VMEM] * (1 + len(arrays)) + [ANY] * len(after),
        out_specs=(VMEM, VMEM),
        out_shape=(
            jax.ShapeDtypeStruct((rows, rank * len(routes)), jnp.float32),
            jax.ShapeDtypeStruct((rank, small_width), tokens.dtype),
        ),
        scratch_shapes=[pltpu.VMEM((rank * len(routes), half), tokens.dtype)],
        compiler_params=params(6),
        cost_estimate=cost(2 * rows * half * rank * len(routes), 2 * rows * half),
        name="shrink",
    )(*routes[0].tables, tokens, *arrays, *after)


def rotary_tables(rows, width):
    half = width // 2
    freqs = np.float32(500000.0) ** (-(np.arange(half, dtype=np.float32) * np.float32(2.0) / np.float32(width)))
    angles = np.arange(rows, dtype=np.float32)[:, None] * freqs.astype(np.float32)[None, :]
    cosine, sine = np.cos(angles), np.sin(angles)
    return (
        np.concatenate([cosine, cosine], axis=1).astype(np.float32),
        np.concatenate([-sine, sine], axis=1).astype(np.float32),
    )


def attention_kernel(
    place, base_own, base_other, shrink_own, shrink_other, small_own, small_other, cosine, sine,
    weight_own, weight_other, out, low_out, *, query_columns, key_columns,
):
    tensor, length = place[0], place[1]
    rank = small_own.shape[0]
    rows = base_own.shape[0]
    size = HEAD_SIZE
    shrink = (shrink_own[...] + shrink_other[...]).astype(jnp.bfloat16)
    first = tensor == 0

    def up(part, base, small, start, base_start, width):
        return base[:, base_start:base_start + width] + jnp.dot(
            part, small[:, start:start + width], preferred_element_type=jnp.float32)

    def rotate(v):
        return v * cosine[...] + pltpu.roll(v, size // 2, 1) * sine[...]

    own_side = shrink[:, rank:2 * rank], shrink[:, 2 * rank:3 * rank]
    own_part = jnp.where(first, own_side[0], own_side[1])
    other_part = jnp.where(first, own_side[1], own_side[0])
    own_kv = up(own_part, base_own, small_own, query_columns, query_columns, key_columns).astype(jnp.bfloat16)
    other_kv = up(other_part, base_other, small_other, query_columns, query_columns, key_columns).astype(jnp.bfloat16)
    keys = jnp.where(first, own_kv, other_kv)
    values = jnp.where(first, other_kv, own_kv)
    keys = rotate(keys.astype(jnp.float32)).astype(jnp.bfloat16)

    at = lax.broadcasted_iota(jnp.int32, (rows, rows), 0)
    to = lax.broadcasted_iota(jnp.int32, (rows, rows), 1)
    allowed = (to <= at) & (to < length)

    def heads(base, small):
        queries = up(shrink[:, :rank], base, small, 0, 0, query_columns)
        done = []
        for start in range(0, query_columns, size):
            query = rotate(queries[:, start:start + size]).astype(jnp.bfloat16)
            scores = lax.dot_general(
                query, keys, (((1,), (1,)), ((), ())), preferred_element_type=jnp.float32) * size ** (-0.5)
            scores = jnp.where(allowed, scores, -1e30)
            expo = jnp.exp(scores - jnp.max(scores, axis=1, keepdims=True))
            weights = (expo / jnp.sum(expo, axis=1, keepdims=True)).astype(jnp.bfloat16)
            done.append(jnp.dot(weights, values, preferred_element_type=jnp.float32).astype(jnp.bfloat16))
        return jnp.concatenate(done, axis=1)

    attended_own = heads(base_own, small_own)
    attended_other = heads(base_other, small_other)

    def down(attended, small):
        return lax.dot_general(
            attended, small[:, query_columns + key_columns:], (((1,), (1,)), ((), ())),
            preferred_element_type=jnp.float32)

    low_out[...] = (down(attended_own, small_own) + down(attended_other, small_other)).astype(jnp.bfloat16)
    tile = 1024
    for start in range(0, out.shape[1], tile):
        cut = slice(start, start + tile)
        own = jnp.dot(attended_own, weight_own[:, cut], preferred_element_type=jnp.float32)
        other = jnp.dot(attended_other, weight_other[:, cut], preferred_element_type=jnp.float32)
        out[:, cut] = own.astype(jnp.bfloat16).astype(jnp.float32) + other.astype(jnp.bfloat16).astype(jnp.float32)


def attention(place, base, shrink, small, weight, query_columns, key_columns):
    rows = base[0].shape[0]
    columns = weight[0].shape[1]
    cosine, sine = rotary_tables(rows, HEAD_SIZE)
    operands = (*base, *shrink, *small, cosine, sine, *weight)
    return pl.pallas_call(
        functools.partial(attention_kernel, query_columns=query_columns, key_columns=key_columns),
        in_specs=[SMEM] + [VMEM] * len(operands),
        out_specs=(VMEM, VMEM),
        out_shape=(
            jax.ShapeDtypeStruct((rows, columns), jnp.float32),
            jax.ShapeDtypeStruct((rows, small[0].shape[0]), jnp.bfloat16),
        ),
        compiler_params=params(8),
        cost_estimate=cost(4 * rows * query_columns * columns, 4 * query_columns * columns),
        name="attention",
    )(place, *operands)


def finish(route, place, base, low):
    rows, columns = base.shape
    arrays = route.arrays()
    tile = 1024

    def kernel(requests, pool, place, base_ref, low_ref, *refs):
        out, up_map, tiles, sems = refs[-4:]

        def store(ref, index):
            up_map[...] = ref[index]

        route.choose((requests, pool), refs[:-4], 0, store)
        valid = lax.broadcasted_iota(jnp.int32, (rows, 1), 0) < place[1]
        copies = []
        for i in range(columns // tile):
            cut = slice(i * tile, (i + 1) * tile)
            delta = jnp.dot(low_ref[...], up_map[:, cut], preferred_element_type=jnp.float32)
            tiles[i] = jnp.where(valid, base_ref[:, cut] + delta, 0.0).astype(tiles.dtype)
            copies.append(pltpu.make_async_copy(tiles.at[i], out.at[:, pl.ds(i * tile, tile)], sems.at[i]))
            copies[-1].start()
        for copy in copies:
            copy.wait()

    return pl.pallas_call(
        kernel,
        in_specs=[SMEM] * 3 + [VMEM] * (2 + len(arrays)),
        out_specs=ANY,
        out_shape=jax.ShapeDtypeStruct((rows, columns), arrays[0].dtype),
        scratch_shapes=[
            pltpu.VMEM(arrays[0].shape[1:], arrays[0].dtype),
            pltpu.VMEM((columns // tile, rows, tile), arrays[0].dtype),
            pltpu.SemaphoreType.DMA((columns // tile,)),
        ],
        compiler_params=params(8),
        cost_estimate=cost(2 * rows * low.shape[1] * columns, 6 * rows * columns),
        name="finish",
    )(*route.tables, place, base, low, *arrays)


def orders(bits):
    each = list(range(bits))
    first = each
    second = [1, 0] + each[2:] if bits > 1 else each
    third = [each[-1]] + each[:-1]
    return first, second, third


def local(
    devices,
    tokens,
    query_weight,
    key_value_weight,
    output_weight,
    adapter_down_maps,
    adapter_query_up,
    adapter_key_value_up,
    adapter_output_down,
    adapter_output_up,
    request_adapter,
    adapter_pool_row,
    lengths,
):
    tensor = lax.axis_index("tensor")
    pair = [(0, 1), (1, 0)]
    half = tokens.shape[1]
    rank = adapter_query_up.shape[1]
    query_columns = query_weight.shape[1]
    key_columns = key_value_weight.shape[1]
    place = jnp.stack([tensor, lengths[0]]).astype(jnp.int32)

    def swap(x):
        return lax.ppermute(x, "tensor", pair)

    small = (adapter_query_up, adapter_key_value_up, adapter_output_down)
    small_width = sum(each.shape[2] for each in small)
    first, second, third = orders(devices.bit_length() - 1)

    def route(part, order):
        return Route(part, order, devices, request_adapter, adapter_pool_row)

    down = [adapter_down_maps[:, i * rank:(i + 1) * rank] for i in range(3)]
    parts = (jnp.concatenate([down[0], *small], axis=2), down[1], down[2])
    first_route, second_route, third_route = (
        route(part, order) for part, order in zip(parts, (first, second, third)))
    routes = [first_route, second_route, third_route]
    up_route = route(adapter_output_up, first)
    weight_other = swap(output_weight)
    other_tokens = swap(tokens)
    for each in (third_route, second_route, first_route, up_route):
        each.step()
    base_own = base_products(tensor, tokens, other_tokens, query_weight, key_value_weight)
    base_other = swap(base_own)
    weight_near, weight_far = (
        lax.dynamic_slice_in_dim(weight, tensor * half, half, 1) for weight in (output_weight, weight_other))
    last = (base_own,)
    turns = (first_route, second_route, third_route, up_route, first_route, second_route, third_route, up_route) * 1
    for turn, each in enumerate(turns):
        if turn == 3:
            last += (weight_near, weight_far)
        sent = each.step(last)
        last = (each.arrays()[-1] if sent is None else sent,)

    shrink_own, small_own = shrink_partial(routes, tokens, small_width, last)
    base, low = attention(
        place, (base_own, base_other), (shrink_own, swap(shrink_own)), (small_own, swap(small_own)),
        (weight_near, weight_far), query_columns, key_columns)
    return finish(up_route, place, base, low)


def solution(mesh):
    placed = (
        P(("group", "serve"), "tensor"),
        P(None, "tensor"),
        P(None, "tensor"),
        P("tensor", None),
        P(("group", "serve"), None, "tensor"),
        P(("group", "serve"), None, "tensor"),
        P(("group", "serve"), None, "tensor"),
        P(("group", "serve"), None, "tensor"),
        P(("group", "serve"), None, "tensor"),
        P("group"),
        P("group"),
        P(("group", "serve")),
    )
    return jax.shard_map(
        functools.partial(local, mesh.shape["serve"]),
        mesh=mesh,
        in_specs=placed,
        out_specs=P(("group", "serve"), "tensor"),
        check_vma=False,
    )
```
